128 devices in a mesh: chan: 8 (over y_lo, x), seq: 16 (over y_hi, z, core).
Axes of the slice: x: 4, y: 4 (y_hi: 2, y_lo: 2; y = y_hi * 2 + y_lo), z: 4, core: 2. Of those that a mesh axis runs over, the one named last changes fastest.
Arguments:
- projected: bfloat16 [3, 32768, 4096], P(None, ('chan', 'seq')), may hold values from -6 to 6
- short_filter: float32 [3, 3, 4096], replicated, may hold values from -3 to 3
- residues: float32 [16, 4096], P(None, ('chan', 'seq')), may hold values from -3 to 3
- decays: float32 [16, 4096], P(None, ('chan', 'seq')), may hold values from 1.5258789e-05 to 0.04
- skip: float32 [4096], P(('chan', 'seq')), may hold values from -4 to 4
Outputs:
- mixed: bfloat16 [32768, 4096], P(('chan', 'seq'))
The draws below stay inside these ranges and needn't reach their ends.
All inputs are finite; a program needn't handle non-finite values.
Results may differ from the reference program's by a relative error of at most 0.01055.
Values may be sent and summed in bfloat16 or wider, within the bound.
A program may use at most 320 MiB of HBM per device.

```python
import math
import jax
import jax.numpy as jnp
from jax import lax

D = 4096
MODES = 16
SEQ = 32768


def levels(stream_key, dims, split, low, top_value):
    def one(dim, blocks):
        steps = jax.random.uniform(jax.random.fold_in(jax.random.fold_in(stream_key, 6), dim), (blocks,), jnp.float32, low / len(split), top_value / len(split))
        return jnp.repeat(jnp.exp(steps), dims[dim] // blocks).reshape((-1,) + (1,) * (len(dims) - dim - 1))

    gain = one(*split[0])
    for cut in split[1:]:
        gain = gain * one(*cut)
    return gain


def noise(key, shape, deviation, reach, cuts=(), kind=jnp.bfloat16):
    loudness = levels(key, shape, cuts, -0.22, 0.18) if cuts else 1.0
    result = jax.random.normal(key, shape, jnp.float32) * deviation * loudness
    return jnp.minimum(jnp.maximum(result, -reach), reach).astype(kind)


def setup_inputs(seed: int = 0) -> dict:
    splits = jax.random.split(jax.random.key(seed), 6)
    return {
        "projected": noise(splits[0], (3, SEQ, D), 1.0, 6.0, ((1, 128),)),
        "short_filter": noise(splits[1], (3, 3, D), 0.6, 3.0, (), jnp.float32),
        "residues": noise(splits[2], (MODES, D), 0.35, 3.0, ((1, 128),), jnp.float32),
        "decays": jnp.clip(jnp.exp(math.log(0.04) - 7.871479 * jax.random.uniform(splits[3], (MODES, D), jnp.float32) ** levels(splits[3], (MODES, D), ((1, 128),), -0.2, 0.2)), 1.52587890625e-05, 0.04),
        "skip": noise(splits[4], (D,), 1.0, 4.0, ((0, 128),), jnp.float32),
    }


def reference(projected, short_filter, residues, decays, skip):
    block_width = 128
    block_count = D // block_width
    times = jnp.arange(SEQ).astype(jnp.float32)
    n_total = 2 * SEQ

    def one_block(block_index):
        start = (block_index * block_width).astype(jnp.int32)
        piece = lax.dynamic_slice_in_dim(projected, start, block_width, 2).astype(jnp.float32)
        filters = lax.dynamic_slice_in_dim(short_filter, start, block_width, 2)
        padded = jnp.pad(piece, ((0, 0), (2, 0), (0, 0)))
        featured = filters[:, 0, None, :] * padded[:, 2:] + filters[:, 1, None, :] * padded[:, 1:-1] + filters[:, 2, None, :] * padded[:, :-2]
        gated = lax.optimization_barrier((featured[1] * featured[2]).astype(jnp.bfloat16)).astype(jnp.float32)
        rates = lax.dynamic_slice_in_dim(decays, start, block_width, 1)
        weights = lax.dynamic_slice_in_dim(residues, start, block_width, 1) * jnp.sqrt(rates)
        taps = lax.optimization_barrier(jnp.sum(weights[:, None, :] * jnp.exp(-rates[:, None, :] * times[None, :, None]), axis=0))
        spectrum = jnp.fft.rfft(gated, n=n_total, axis=0) * jnp.fft.rfft(taps, n=n_total, axis=0)
        direct = lax.dynamic_slice_in_dim(skip, start, block_width, 0)
        conv = jnp.fft.irfft(spectrum, n=n_total, axis=0)[:SEQ] + direct[None, :] * gated
        conv = lax.optimization_barrier(conv.astype(jnp.bfloat16)).astype(jnp.float32)
        return (featured[0] * conv).astype(jnp.bfloat16)
    blocks = lax.map(one_block, jnp.arange(block_count).astype(jnp.int32))
    return blocks.transpose(1, 0, 2).reshape(SEQ, D)
```

```python
import functools

import jax
import jax.numpy as jnp
from jax import lax
from jax.experimental import pallas as pl
from jax.experimental.pallas import tpu as pltpu
from jax.sharding import PartitionSpec as P

LANES = 128
ROWS = 8
WIDE = LANES * ROWS
BLOCK = 8
PAIR = 16
MESH = pl.DeviceIdType.MESH
F32 = jnp.float32


def token(t):
    return pl.ds((t // ROWS) * ROWS * ROWS + t % ROWS, ROWS, stride=ROWS)


def kernel(
    n_chan,
    n_seq,
    x_hbm,
    filt,
    weight,
    decay,
    skip,
    halo,
    out_hbm,
    xb,
    tiles,
    gated,
    queries,
    ends,
    power,
    power_block,
    taps,
    state,
    got_state,
    before,
    total,
    got_total,
    back,
    carried,
    out_tiles,
    out_rows,
    in_sem,
    out_sem,
    send_state,
    recv_state,
    send_total,
    recv_total,
    send_back,
    recv_back,
):
    groups = gated.shape[0]
    length = x_hbm.shape[1]
    modes = weight.shape[0]
    my_chan = lax.axis_index("chan")
    my_seq = lax.axis_index("seq")

    def fetch(j, m):
        columns = pl.ds(m * WIDE, WIDE)
        return pltpu.make_async_copy(
            x_hbm.at[j, :, columns], xb.at[j, :, columns], in_sem.at[m, j]
        )

    for m in range(groups):
        for j in range(3):
            fetch(j, m).start()

    barrier = pltpu.get_barrier_semaphore()
    for off in range(1, n_seq):
        peer = lax.rem(my_seq + off, n_seq)
        pl.semaphore_signal(barrier, inc=1, device_id=(my_chan, peer), device_id_type=MESH)
    for off in range(1, n_chan):
        peer = lax.rem(my_chan + off, n_chan)
        pl.semaphore_signal(barrier, inc=1, device_id=(peer, my_seq), device_id_type=MESH)

    power[...] = jnp.exp(-decay[...])
    power_block[...] = jnp.exp(-float(BLOCK) * decay[...])

    def feature(m):
        for j in range(3):
            fetch(j, m).wait()
        coefs = [[filt[3 * j + s, m] for s in range(3)] for j in range(3)]

        def step(b, olds):
            for j in range(3):
                rows = xb[j, pl.ds(pl.multiple_of(b * PAIR, PAIR), PAIR), m * WIDE : (m + 1) * WIDE]
                rows = rows.astype(F32)
                for h in range(PAIR // ROWS):
                    for i in range(ROWS):
                        at = (h * ROWS + i) * ROWS
                        tiles[j, at : at + ROWS, :] = rows[
                            h * ROWS : (h + 1) * ROWS, i * LANES : (i + 1) * LANES
                        ]
            olds = list(olds)
            for t in range(PAIR):
                featured = []
                for j in range(3):
                    now = tiles[j, token(t), :]
                    older, old = olds[2 * j], olds[2 * j + 1]
                    featured.append(coefs[j][0] * now + coefs[j][1] * old + coefs[j][2] * older)
                    olds[2 * j], olds[2 * j + 1] = old, now
                place = pl.ds(pl.multiple_of((b * PAIR + t) * ROWS, ROWS), ROWS)
                queries[m, place, :] = featured[0]
                gated[m, place, :] = featured[1] * featured[2]
            return tuple(olds)

        lax.fori_loop(0, length // PAIR, step, tuple(halo[i, m] for i in range(6)))

    def gather_states(m):
        def step(b, states):
            values = [
                gated[m, pl.ds(pl.multiple_of((b * BLOCK + i) * ROWS, ROWS), ROWS), :]
                for i in range(BLOCK)
            ]
            results = []
            for n in range(modes):
                rate = power[n, m]
                end = values[0]
                for i in range(1, BLOCK):
                    end = rate * end + values[i]
                end = weight[n, m] * end
                ends[m, b, n] = end
                results.append(power_block[n, m] * states[n] + end)
            return tuple(results)

        zero = jnp.zeros((ROWS, LANES), F32)
        states = lax.fori_loop(0, length // BLOCK, step, (zero,) * modes)
        for n in range(modes):
            state[m, n] = states[n]

    def state_copy(m, off):
        peer = lax.rem(my_seq + off, n_seq)
        return pltpu.make_async_remote_copy(
            src_ref=state.at[m, peer],
            dst_ref=got_state.at[m, my_seq],
            send_sem=send_state.at[m],
            recv_sem=recv_state.at[m],
            device_id=(my_chan, peer),
            device_id_type=MESH,
        )

    def total_copy(m, off):
        peer = lax.rem(my_chan + off, n_chan)
        return pltpu.make_async_remote_copy(
            src_ref=total.at[m],
            dst_ref=got_total.at[m, my_chan],
            send_sem=send_total.at[m],
            recv_sem=recv_total.at[m],
            device_id=(peer, my_seq),
            device_id_type=MESH,
        )

    def back_copy(m, off):
        peer = lax.rem(my_seq + off, n_seq)
        return pltpu.make_async_remote_copy(
            src_ref=back.at[m, peer],
            dst_ref=carried.at[m, my_seq],
            send_sem=send_back.at[m],
            recv_sem=recv_back.at[m],
            device_id=(my_chan, peer),
            device_id_type=MESH,
        )

    def wait_bytes(ref, count, m, sem):
        some = ref.at[m, pl.ds(0, count)]
        pltpu.make_async_copy(some, some, sem.at[m]).wait()

    def send_states(m):
        for off in range(1, n_seq):
            state_copy(m, off).start()
        got_state[m, my_seq] = state[m, my_seq]

    def scan_group(m):
        wait_bytes(got_state, n_seq - 1, m, recv_state)
        shrink = jnp.exp(-float(length) * decay[my_seq, m])
        running = jnp.zeros((ROWS, LANES), F32)
        for k in range(n_seq):
            before[m, k] = running
            running = shrink * running + got_state[m, k]
        total[m] = running
        for off in range(1, n_chan):
            total_copy(m, off).start()

    def scan_all(m):
        wait_bytes(got_total, n_chan - 1, m, recv_total)
        rate = decay[my_seq, m]
        shrink = jnp.exp(-float(length) * rate)
        shrink_group = jnp.exp(-float(length * n_seq) * rate)
        running = jnp.zeros((ROWS, LANES), F32)
        for c in range(n_chan - 1):
            running = jnp.where(c < my_chan, shrink_group * running + got_total[m, c], running)
        for k in range(n_seq):
            back[m, k] = before[m, k] + running
            running = shrink * running
        for off in range(1, n_seq):
            back_copy(m, off).start()
        carried[m, my_seq] = back[m, my_seq]

    def write(m):
        columns = pl.ds(m * WIDE, WIDE)
        return pltpu.make_async_copy(out_rows.at[:, columns], out_hbm.at[:, columns], out_sem.at[m])

    def convolve(m):
        wait_bytes(carried, n_seq - 1, m, recv_back)
        term = [weight[n, m] for n in range(modes)]
        for i in range(BLOCK):
            tap = term[0]
            for n in range(1, modes):
                tap = tap + term[n]
            taps[i] = tap + skip[m] if i == 0 else tap
            if i < BLOCK - 1:
                term = [term[n] * power[n, m] for n in range(modes)]

        def step(pair, states):
            for half in range(PAIR // BLOCK):
                b = pair * (PAIR // BLOCK) + half
                places = [
                    pl.ds(pl.multiple_of((b * BLOCK + i) * ROWS, ROWS), ROWS) for i in range(BLOCK)
                ]
                values = [gated[m, places[i], :] for i in range(BLOCK)]
                sums = []
                for i in range(BLOCK):
                    one = taps[0] * values[i]
                    for j in range(1, i + 1):
                        one = one + taps[j] * values[i - j]
                    sums.append(one)
                results = []
                for n in range(modes):
                    rate = power[n, m]
                    now = states[n]
                    for i in range(BLOCK):
                        now = now * rate
                        sums[i] = sums[i] + now
                    results.append(now + ends[m, b, n])
                states = tuple(results)
                for i in range(BLOCK):
                    out_tiles[token(half * BLOCK + i), :] = sums[i] * queries[m, places[i], :]
            for i in range(ROWS):
                parts = [
                    out_tiles[(h * ROWS + i) * ROWS : (h * ROWS + i + 1) * ROWS, :]
                    for h in range(PAIR // ROWS)
                ]
                lanes = m * WIDE + i * LANES
                out_rows[pl.ds(pl.multiple_of(pair * PAIR, PAIR), PAIR), lanes : lanes + LANES] = (
                    jnp.concatenate(parts, axis=0).astype(out_rows.dtype)
                )
            return states

        lax.fori_loop(0, length // PAIR, step, tuple(carried[m, n] for n in range(modes)))
        write(m).start()

    for m in range(groups):
        feature(m)
    pl.semaphore_wait(barrier, n_seq + n_chan - 2)
    for m in range(groups):
        gather_states(m)
        send_states(m)
        if m >= 1:
            scan_group(m - 1)
        if m >= 2:
            scan_all(m - 2)
    for m in range(groups):
        convolve(m)
        if m == 0:
            scan_group(groups - 1)
            scan_all(groups - 2)
        if m == 1:
            scan_all(groups - 1)
    for m in range(groups):
        write(m).wait()
        wait_bytes(got_state, n_seq - 1, m, send_state)
        wait_bytes(got_total, n_chan - 1, m, send_total)
        wait_bytes(carried, n_seq - 1, m, send_back)


def shards(n_chan, n_seq, projected, short_filter, residues, decays, skip):
    _, length, width = projected.shape
    modes = residues.shape[0]
    groups = width // WIDE
    axes = ("chan", "seq")
    packed = jnp.concatenate([residues * jnp.sqrt(decays), decays, skip[None]], axis=0)
    params = lax.all_gather(packed, axes, axis=1, tiled=True)
    params = params.reshape(2 * modes + 1, groups, ROWS, LANES)
    count = n_chan * n_seq
    halo = lax.ppermute(projected[:, -2:, :], axes, [(i, i + 1) for i in range(count - 1)])
    halo = halo.astype(F32).reshape(6, groups, ROWS, LANES)
    filt = short_filter.reshape(9, groups, ROWS, LANES)
    vmem = pl.BlockSpec(memory_space=pltpu.VMEM)
    hbm = pl.BlockSpec(memory_space=pl.ANY)
    dma = pltpu.SemaphoreType.DMA
    blocks = length // BLOCK
    return pl.pallas_call(
        functools.partial(kernel, n_chan, n_seq),
        out_shape=jax.ShapeDtypeStruct((length, width), projected.dtype),
        in_specs=[hbm] + [vmem] * 5,
        out_specs=hbm,
        scratch_shapes=[
            pltpu.VMEM((3, length, width), projected.dtype),
            pltpu.VMEM((3, PAIR * ROWS, LANES), F32),
            pltpu.VMEM((groups, length * ROWS, LANES), F32),
            pltpu.VMEM((groups, length * ROWS, LANES), F32),
            pltpu.VMEM((groups, blocks, modes, ROWS, LANES), F32),
            pltpu.VMEM((modes, groups, ROWS, LANES), F32),
            pltpu.VMEM((modes, groups, ROWS, LANES), F32),
            pltpu.VMEM((BLOCK, ROWS, LANES), F32),
            pltpu.VMEM((groups, modes, ROWS, LANES), F32),
            pltpu.VMEM((groups, n_seq, ROWS, LANES), F32),
            pltpu.VMEM((groups, n_seq, ROWS, LANES), F32),
            pltpu.VMEM((groups, ROWS, LANES), F32),
            pltpu.VMEM((groups, n_chan, ROWS, LANES), F32),
            pltpu.VMEM((groups, n_seq, ROWS, LANES), F32),
            pltpu.VMEM((groups, modes, ROWS, LANES), F32),
            pltpu.VMEM((PAIR * ROWS, LANES), F32),
            pltpu.VMEM((length, width), projected.dtype),
            dma((groups, 3)),
            dma((groups,)),
            dma((groups,)),
            dma((groups,)),
            dma((groups,)),
            dma((groups,)),
            dma((groups,)),
            dma((groups,)),
        ],
        compiler_params=pltpu.CompilerParams(
            collective_id=0, has_side_effects=True, vmem_limit_bytes=48 * 1024 * 1024
        ),
        name="hyena",
    )(projected, filt, params[:modes], params[modes : 2 * modes], params[2 * modes], halo)


def solution(mesh):
    return jax.shard_map(
        functools.partial(shards, mesh.shape["chan"], mesh.shape["seq"]),
        mesh=mesh,
        in_specs=(
            P(None, ("chan", "seq"), None),
            P(),
            P(None, ("chan", "seq")),
            P(None, ("chan", "seq")),
            P(("chan", "seq")),
        ),
        out_specs=P(("chan", "seq"), None),
        check_vma=False,
    )
```

```python
import functools

import jax
import jax.numpy as jnp
from jax import lax
from jax.experimental import pallas as pl
from jax.experimental.pallas import tpu as pltpu
from jax.sharding import PartitionSpec as P

LANES = 128
ROWS = 8
WIDE = LANES * ROWS
BLOCK = 8
PAIR = 16
MESH = pl.DeviceIdType.MESH
F32 = jnp.float32


def token(t):
    return pl.ds((t // ROWS) * ROWS * ROWS + t % ROWS, ROWS, stride=ROWS)


def kernel(
    n_chan,
    n_seq,
    x_hbm,
    filt,
    residues,
    rates,
    direct,
    out_hbm,
    xb,
    tiles,
    gated,
    queries,
    ends,
    params,
    weight,
    decay,
    skip,
    last,
    halo,
    head,
    power,
    power_block,
    taps,
    state,
    got_state,
    before,
    total,
    got_total,
    back,
    carried,
    out_tiles,
    out_rows,
    in_sem,
    out_sem,
    send_near,
    recv_near,
    send_far,
    recv_far,
    send_halo,
    recv_halo,
    send_state,
    recv_state,
    send_total,
    recv_total,
    send_back,
    recv_back,
):
    groups = gated.shape[0]
    length = x_hbm.shape[1]
    modes = weight.shape[0]
    share = n_chan // groups
    my_chan = lax.axis_index("chan")
    my_seq = lax.axis_index("seq")
    count = n_chan * n_seq
    mine = my_chan * n_seq + my_seq
    after = lax.rem(mine + 1, count)
    ahead = lax.rem(mine + count - 1, count)

    def fetch(j, m):
        columns = pl.ds(m * WIDE, WIDE)
        return pltpu.make_async_copy(
            x_hbm.at[j, :, columns], xb.at[j, :, columns], in_sem.at[m, j]
        )

    for m in range(groups):
        for j in range(3):
            fetch(j, m).start()

    barrier = pltpu.get_barrier_semaphore()
    for off in range(1, n_seq):
        peer = lax.rem(my_seq + off, n_seq)
        pl.semaphore_signal(barrier, inc=1, device_id=(my_chan, peer), device_id_type=MESH)
    for off in range(1, n_chan):
        peer = lax.rem(my_chan + off, n_chan)
        pl.semaphore_signal(barrier, inc=1, device_id=(peer, my_seq), device_id_type=MESH)
    pl.semaphore_signal(
        barrier, inc=1, device_id=(ahead // n_seq, ahead % n_seq), device_id_type=MESH
    )

    part = residues.shape[1]
    quads = LANES // part
    half = modes // quads
    for r in range(half):
        for b in range(quads):
            n = r * quads + b
            lanes = slice(b * part, (b + 1) * part)
            params[mine, r : r + 1, lanes] = residues[n : n + 1, :] * jnp.sqrt(rates[n : n + 1, :])
            params[mine, half + r : half + r + 1, lanes] = rates[n : n + 1, :]
    params[mine, 2 * half : 2 * half + 1, 0:part] = direct[...]
    params[mine, 2 * half : 2 * half + 1, part:] = jnp.zeros((1, LANES - part), F32)

    def near_copy(off):
        peer = lax.rem(my_chan + off, n_chan)
        return pltpu.make_async_remote_copy(
            src_ref=params.at[mine],
            dst_ref=params.at[mine],
            send_sem=send_near,
            recv_sem=recv_near,
            device_id=(peer, my_seq),
            device_id_type=MESH,
        )

    def far_copy(c, off):
        peer = lax.rem(my_seq + off, n_seq)
        place = params.at[c * n_seq + my_seq]
        return pltpu.make_async_remote_copy(
            src_ref=place,
            dst_ref=place,
            send_sem=send_far.at[c // share],
            recv_sem=recv_far.at[c // share],
            device_id=(my_chan, peer),
            device_id_type=MESH,
        )

    def halo_copy(m):
        return pltpu.make_async_remote_copy(
            src_ref=last.at[m],
            dst_ref=halo.at[m],
            send_sem=send_halo.at[m],
            recv_sem=recv_halo.at[m],
            device_id=(after // n_seq, after % n_seq),
            device_id_type=MESH,
        )

    def spread_params(m):
        some = params.at[pl.ds(0, (n_seq - 1) * share)]
        pltpu.make_async_copy(some, some, recv_far.at[m]).wait()
        group = lax.broadcasted_iota(jnp.int32, (ROWS, LANES), 1) // part
        depth = params.shape[1]

        def pick(row):
            found = []
            for i in range(quads):
                found.append(
                    jnp.concatenate(
                        [
                            params[(m * ROWS + j) * quads + i, row : row + 1, :]
                            for j in range(ROWS)
                        ],
                        axis=0,
                    )
                )
            return found

        def place(found, b):
            value = None
            for i in range(quads):
                shift = (i - b) % quads * part
                turned = pltpu.roll(found[i], shift, 1) if shift else found[i]
                value = turned if i == 0 else jnp.where(group == i, turned, value)
            return value

        for r in range(half):
            heavy = pick(r)
            rate = pick(half + r)
            for b in range(quads):
                n = r * quads + b
                weight[n, m] = place(heavy, b)
                value = place(rate, b)
                decay[n, m] = value
                power[n, m] = jnp.exp(-value)
                power_block[n, m] = jnp.exp(-float(BLOCK) * value)
        skip[m] = place(pick(2 * half), 0)

    def patch(m):
        halo_copy(m).wait_recv()
        for t in range(2):
            featured = []
            for j in range(3):
                rows = [
                    jnp.where(mine > 0, halo[m, 2 * j], 0.0),
                    jnp.where(mine > 0, halo[m, 2 * j + 1], 0.0),
                    head[m, 2 * j],
                    head[m, 2 * j + 1],
                ]
                featured.append(
                    filt[3 * j, m] * rows[t + 2]
                    + filt[3 * j + 1, m] * rows[t + 1]
                    + filt[3 * j + 2, m] * rows[t]
                )
            queries[m, t * ROWS : (t + 1) * ROWS, :] = featured[0]
            gated[m, t * ROWS : (t + 1) * ROWS, :] = featured[1] * featured[2]

    def feature(m):
        for j in range(3):
            fetch(j, m).wait()
        coefs = [[filt[3 * j + s, m] for s in range(3)] for j in range(3)]

        def step(b, olds):
            for j in range(3):
                rows = xb[j, pl.ds(pl.multiple_of(b * PAIR, PAIR), PAIR), m * WIDE : (m + 1) * WIDE]
                rows = rows.astype(F32)
                for h in range(PAIR // ROWS):
                    for i in range(ROWS):
                        at = (h * ROWS + i) * ROWS
                        tiles[j, at : at + ROWS, :] = rows[
                            h * ROWS : (h + 1) * ROWS, i * LANES : (i + 1) * LANES
                        ]
            olds = list(olds)
            for t in range(PAIR):
                featured = []
                for j in range(3):
                    now = tiles[j, token(t), :]
                    older, old = olds[2 * j], olds[2 * j + 1]
                    featured.append(coefs[j][0] * now + coefs[j][1] * old + coefs[j][2] * older)
                    olds[2 * j], olds[2 * j + 1] = old, now
                place = pl.ds(pl.multiple_of((b * PAIR + t) * ROWS, ROWS), ROWS)
                queries[m, place, :] = featured[0]
                gated[m, place, :] = featured[1] * featured[2]
            return tuple(olds)

        zero = jnp.zeros((ROWS, LANES), F32)
        olds = lax.fori_loop(0, length // PAIR, step, (zero,) * 6)
        for i in range(6):
            last[m, i] = olds[i]
        halo_copy(m).start()
        for j in range(3):
            rows = xb[j, 0:PAIR, m * WIDE : (m + 1) * WIDE].astype(F32)[:ROWS]
            for i in range(ROWS):
                tiles[j, i * ROWS : (i + 1) * ROWS, :] = rows[:, i * LANES : (i + 1) * LANES]
            for t in range(2):
                head[m, 2 * j + t] = tiles[j, token(t), :]

    def gather_states(m):
        def step(b, states):
            values = [
                gated[m, pl.ds(pl.multiple_of((b * BLOCK + i) * ROWS, ROWS), ROWS), :]
                for i in range(BLOCK)
            ]
            results = []
            for n in range(modes):
                rate = power[n, m]
                end = values[0]
                for i in range(1, BLOCK):
                    end = rate * end + values[i]
                end = weight[n, m] * end
                ends[m, b, n] = end
                results.append(power_block[n, m] * states[n] + end)
            return tuple(results)

        zero = jnp.zeros((ROWS, LANES), F32)
        states = lax.fori_loop(0, length // BLOCK, step, (zero,) * modes)
        for n in range(modes):
            state[m, n] = states[n]

    def state_copy(m, off):
        peer = lax.rem(my_seq + off, n_seq)
        return pltpu.make_async_remote_copy(
            src_ref=state.at[m, peer],
            dst_ref=got_state.at[m, my_seq],
            send_sem=send_state.at[m],
            recv_sem=recv_state.at[m],
            device_id=(my_chan, peer),
            device_id_type=MESH,
        )

    def total_copy(m, off):
        peer = lax.rem(my_chan + off, n_chan)
        return pltpu.make_async_remote_copy(
            src_ref=total.at[m],
            dst_ref=got_total.at[m, my_chan],
            send_sem=send_total.at[m],
            recv_sem=recv_total.at[m],
            device_id=(peer, my_seq),
            device_id_type=MESH,
        )

    def back_copy(m, off):
        peer = lax.rem(my_seq + off, n_seq)
        return pltpu.make_async_remote_copy(
            src_ref=back.at[m, peer],
            dst_ref=carried.at[m, my_seq],
            send_sem=send_back.at[m],
            recv_sem=recv_back.at[m],
            device_id=(my_chan, peer),
            device_id_type=MESH,
        )

    def wait_bytes(ref, count, m, sem):
        some = ref.at[m, pl.ds(0, count)]
        pltpu.make_async_copy(some, some, sem.at[m]).wait()

    def send_states(m):
        for off in range(1, n_seq):
            state_copy(m, off).start()
        got_state[m, my_seq] = state[m, my_seq]

    def scan_group(m):
        wait_bytes(got_state, n_seq - 1, m, recv_state)
        shrink = jnp.exp(-float(length) * decay[my_seq, m])
        running = jnp.zeros((ROWS, LANES), F32)
        for k in range(n_seq):
            before[m, k] = running
            running = shrink * running + got_state[m, k]
        total[m] = running
        for off in range(1, n_chan):
            total_copy(m, off).start()

    def scan_all(m):
        wait_bytes(got_total, n_chan - 1, m, recv_total)
        rate = decay[my_seq, m]
        shrink = jnp.exp(-float(length) * rate)
        shrink_group = jnp.exp(-float(length * n_seq) * rate)
        running = jnp.zeros((ROWS, LANES), F32)
        for c in range(n_chan - 1):
            running = jnp.where(c < my_chan, shrink_group * running + got_total[m, c], running)
        for k in range(n_seq):
            back[m, k] = before[m, k] + running
            running = shrink * running
        for off in range(1, n_seq):
            back_copy(m, off).start()
        carried[m, my_seq] = back[m, my_seq]

    def write(m):
        columns = pl.ds(m * WIDE, WIDE)
        return pltpu.make_async_copy(out_rows.at[:, columns], out_hbm.at[:, columns], out_sem.at[m])

    def convolve(m):
        wait_bytes(carried, n_seq - 1, m, recv_back)
        term = [weight[n, m] for n in range(modes)]
        for i in range(BLOCK):
            tap = term[0]
            for n in range(1, modes):
                tap = tap + term[n]
            taps[i] = tap + skip[m] if i == 0 else tap
            if i < BLOCK - 1:
                term = [term[n] * power[n, m] for n in range(modes)]

        def step(pair, states):
            for half in range(PAIR // BLOCK):
                b = pair * (PAIR // BLOCK) + half
                places = [
                    pl.ds(pl.multiple_of((b * BLOCK + i) * ROWS, ROWS), ROWS) for i in range(BLOCK)
                ]
                values = [gated[m, places[i], :] for i in range(BLOCK)]
                sums = []
                for i in range(BLOCK):
                    one = taps[0] * values[i]
                    for j in range(1, i + 1):
                        one = one + taps[j] * values[i - j]
                    sums.append(one)
                results = []
                for n in range(modes):
                    rate = power[n, m]
                    now = states[n]
                    for i in range(BLOCK):
                        now = now * rate
                        sums[i] = sums[i] + now
                    results.append(now + ends[m, b, n])
                states = tuple(results)
                for i in range(BLOCK):
                    out_tiles[token(half * BLOCK + i), :] = sums[i] * queries[m, places[i], :]
            for i in range(ROWS):
                parts = [
                    out_tiles[(h * ROWS + i) * ROWS : (h * ROWS + i + 1) * ROWS, :]
                    for h in range(PAIR // ROWS)
                ]
                lanes = m * WIDE + i * LANES
                out_rows[pl.ds(pl.multiple_of(pair * PAIR, PAIR), PAIR), lanes : lanes + LANES] = (
                    jnp.concatenate(parts, axis=0).astype(out_rows.dtype)
                )
            return states

        lax.fori_loop(0, length // PAIR, step, tuple(carried[m, n] for n in range(modes)))
        write(m).start()

    pl.semaphore_wait(barrier, n_seq + n_chan - 1)
    for off in range(1, n_chan):
        near_copy(off).start()
    for m in range(groups):
        feature(m)
        if m == 0:
            some = params.at[pl.ds(0, n_chan - 1)]
            pltpu.make_async_copy(some, some, recv_near).wait()
            for c in range(n_chan):
                for off in range(1, n_seq):
                    far_copy(c, off).start()
    for m in range(groups):
        patch(m)
        spread_params(m)
        gather_states(m)
        send_states(m)
        if m >= 1:
            scan_group(m - 1)
        if m >= 2:
            scan_all(m - 2)
    for m in range(groups):
        convolve(m)
        if m == 0:
            scan_group(groups - 1)
            scan_all(groups - 2)
        if m == 1:
            scan_all(groups - 1)
    some = params.at[pl.ds(0, n_chan - 1)]
    pltpu.make_async_copy(some, some, send_near).wait()
    some = params.at[pl.ds(0, (n_seq - 1) * share)]
    for m in range(groups):
        write(m).wait()
        halo_copy(m).wait_send()
        pltpu.make_async_copy(some, some, send_far.at[m]).wait()
        wait_bytes(got_state, n_seq - 1, m, send_state)
        wait_bytes(got_total, n_chan - 1, m, send_total)
        wait_bytes(carried, n_seq - 1, m, send_back)


def shards(n_chan, n_seq, projected, short_filter, residues, decays, skip):
    _, length, width = projected.shape
    modes = residues.shape[0]
    groups = width // WIDE
    filt = short_filter.reshape(9, groups, ROWS, LANES)
    vmem = pl.BlockSpec(memory_space=pltpu.VMEM)
    hbm = pl.BlockSpec(memory_space=pl.ANY)
    dma = pltpu.SemaphoreType.DMA
    blocks = length // BLOCK
    return pl.pallas_call(
        functools.partial(kernel, n_chan, n_seq),
        out_shape=jax.ShapeDtypeStruct((length, width), projected.dtype),
        in_specs=[hbm] + [vmem] * 4,
        out_specs=hbm,
        scratch_shapes=[
            pltpu.VMEM((3, length, width), projected.dtype),
            pltpu.VMEM((3, PAIR * ROWS, LANES), F32),
            pltpu.VMEM((groups, length * ROWS, LANES), F32),
            pltpu.VMEM((groups, length * ROWS, LANES), F32),
            pltpu.VMEM((groups, blocks, modes, ROWS, LANES), F32),
            pltpu.VMEM((n_chan * n_seq, 2 * ROWS, LANES), F32),
            pltpu.VMEM((modes, groups, ROWS, LANES), F32),
            pltpu.VMEM((modes, groups, ROWS, LANES), F32),
            pltpu.VMEM((groups, ROWS, LANES), F32),
            pltpu.VMEM((groups, 6, ROWS, LANES), F32),
            pltpu.VMEM((groups, 6, ROWS, LANES), F32),
            pltpu.VMEM((groups, 6, ROWS, LANES), F32),
            pltpu.VMEM((modes, groups, ROWS, LANES), F32),
            pltpu.VMEM((modes, groups, ROWS, LANES), F32),
            pltpu.VMEM((BLOCK, ROWS, LANES), F32),
            pltpu.VMEM((groups, modes, ROWS, LANES), F32),
            pltpu.VMEM((groups, n_seq, ROWS, LANES), F32),
            pltpu.VMEM((groups, n_seq, ROWS, LANES), F32),
            pltpu.VMEM((groups, ROWS, LANES), F32),
            pltpu.VMEM((groups, n_chan, ROWS, LANES), F32),
            pltpu.VMEM((groups, n_seq, ROWS, LANES), F32),
            pltpu.VMEM((groups, modes, ROWS, LANES), F32),
            pltpu.VMEM((PAIR * ROWS, LANES), F32),
            pltpu.VMEM((length, width), projected.dtype),
            dma((groups, 3)),
            dma((groups,)),
            dma,
            dma,
            dma((groups,)),
            dma((groups,)),
            dma((groups,)),
            dma((groups,)),
            dma((groups,)),
            dma((groups,)),
            dma((groups,)),
            dma((groups,)),
            dma((groups,)),
            dma((groups,)),
        ],
        compiler_params=pltpu.CompilerParams(
            collective_id=0, has_side_effects=True, vmem_limit_bytes=48 * 1024 * 1024
        ),
        name="hyena",
    )(projected, filt, residues, decays, skip[None])


def solution(mesh):
    return jax.shard_map(
        functools.partial(shards, mesh.shape["chan"], mesh.shape["seq"]),
        mesh=mesh,
        in_specs=(
            P(None, ("chan", "seq"), None),
            P(),
            P(None, ("chan", "seq")),
            P(None, ("chan", "seq")),
            P(("chan", "seq")),
        ),
        out_specs=P(("chan", "seq"), None),
        check_vma=False,
    )
```

```python
import functools

import jax
import jax.numpy as jnp
from jax import lax
from jax.experimental import pallas as pl
from jax.experimental.pallas import tpu as pltpu
from jax.sharding import PartitionSpec as P

LANES = 128
ROWS = 8
WIDE = LANES * ROWS
BLOCK = 8
PAIR = 16
MESH = pl.DeviceIdType.MESH
F32 = jnp.float32


def token(t):
    return pl.ds((t // ROWS) * ROWS * ROWS + t % ROWS, ROWS, stride=ROWS)


def kernel(
    n_chan,
    n_seq,
    x_hbm,
    filt_hbm,
    residues_hbm,
    rates_hbm,
    direct_hbm,
    out_hbm,
    xb,
    filt_rows,
    filt,
    residues,
    rates,
    direct,
    tiles,
    gated,
    queries,
    ends,
    params,
    weight,
    decay,
    skip,
    last,
    halo,
    head,
    power,
    power_block,
    taps,
    state,
    got_state,
    before,
    total,
    got_total,
    back,
    carried,
    out_tiles,
    out_rows,
    in_sem,
    small_sem,
    out_sem,
    send_near,
    recv_near,
    send_far,
    recv_far,
    send_halo,
    recv_halo,
    send_state,
    recv_state,
    send_total,
    recv_total,
    send_back,
    recv_back,
):
    groups = gated.shape[0]
    length = x_hbm.shape[1]
    modes = weight.shape[0]
    my_chan = lax.axis_index("chan")
    my_seq = lax.axis_index("seq")
    count = n_chan * n_seq
    mine = my_chan * n_seq + my_seq
    after = lax.rem(mine + 1, count)
    ahead = lax.rem(mine + count - 1, count)

    def fetch(j, m):
        columns = pl.ds(m * WIDE, WIDE)
        return pltpu.make_async_copy(
            x_hbm.at[j, :, columns], xb.at[j, :, columns], in_sem.at[m, j]
        )

    small = [
        pltpu.make_async_copy(source, place, small_sem.at[i])
        for i, (source, place) in enumerate(
            [
                (residues_hbm, residues),
                (rates_hbm, rates),
                (direct_hbm, direct),
                (filt_hbm, filt_rows),
            ]
        )
    ]
    for copy in small:
        copy.start()
    for m in range(groups):
        for j in range(3):
            fetch(j, m).start()

    chips = count // 2
    my_chip = mine // 2
    my_core = mine % 2
    other = 1 - my_core

    def device(chip, core):
        per = n_seq // 2
        return chip // per, chip % per * 2 + core

    def signal(target):
        pl.semaphore_signal(barrier, inc=1, device_id=target, device_id_type=MESH)

    barrier = pltpu.get_barrier_semaphore()
    for off in range(1, chips):
        signal(device(lax.rem(my_chip + off, chips), my_core))
    first_chip = my_chip - my_chip % (n_seq // 2)
    for off in range(n_seq // 2):
        signal(device(first_chip + off, other))
    signal((ahead // n_seq, ahead % n_seq))
    signals = chips - 1 + n_seq // 2 + 1

    for copy in small:
        copy.wait()
    for j in range(3):
        for tap in range(3):
            for m in range(groups):
                for i in range(ROWS):
                    lanes = slice(m * WIDE + i * LANES, m * WIDE + (i + 1) * LANES)
                    filt[3 * j + tap, m, i : i + 1, :] = filt_rows[j, tap : tap + 1, lanes]

    part = residues.shape[1]
    quads = LANES // part
    half = modes // quads
    for r in range(half):
        for b in range(quads):
            n = r * quads + b
            lanes = slice(b * part, (b + 1) * part)
            params[my_chip, my_core, r : r + 1, lanes] = residues[n : n + 1, :] * jnp.sqrt(rates[n : n + 1, :])
            params[my_chip, my_core, half + r : half + r + 1, lanes] = rates[n : n + 1, :]
    params[my_chip, my_core, 2 * half : 2 * half + 1, 0:part] = direct[...]
    params[my_chip, my_core, 2 * half : 2 * half + 1, part:] = jnp.zeros((1, LANES - part), F32)

    used = pl.ds(0, 2 * half + 1)

    def near_copy(off):
        place = params.at[my_chip, my_core, used]
        return pltpu.make_async_remote_copy(
            src_ref=place,
            dst_ref=place,
            send_sem=send_near,
            recv_sem=recv_near,
            device_id=device(lax.rem(my_chip + off, chips), my_core),
            device_id_type=MESH,
        )

    def wait_near(sem):
        some = params.at[pl.ds(0, chips - 1), 0, used]
        pltpu.make_async_copy(some, some, sem).wait()

    def far_copy(m):
        place = params.at[pl.ds(m * (chips // groups), chips // groups), my_core, used]
        return pltpu.make_async_remote_copy(
            src_ref=place,
            dst_ref=place,
            send_sem=send_far.at[m],
            recv_sem=recv_far.at[m],
            device_id=device(my_chip, other),
            device_id_type=MESH,
        )

    def halo_copy(m):
        return pltpu.make_async_remote_copy(
            src_ref=last.at[m],
            dst_ref=halo.at[m],
            send_sem=send_halo.at[m],
            recv_sem=recv_halo.at[m],
            device_id=(after // n_seq, after % n_seq),
            device_id_type=MESH,
        )

    def spread_params(m):
        far_copy(m).wait_recv()
        group = lax.broadcasted_iota(jnp.int32, (ROWS, LANES), 1) // part

        def pick(row):
            found = []
            for i in range(quads):
                found.append(
                    jnp.concatenate(
                        [
                            params[((m * ROWS + j) * quads + i) // 2, i % 2, row : row + 1, :]
                            for j in range(ROWS)
                        ],
                        axis=0,
                    )
                )
            return found

        def place(found, b):
            value = None
            for i in range(quads):
                shift = (i - b) % quads * part
                turned = pltpu.roll(found[i], shift, 1) if shift else found[i]
                value = turned if i == 0 else jnp.where(group == i, turned, value)
            return value

        for r in range(half):
            heavy = pick(r)
            rate = pick(half + r)
            for b in range(quads):
                n = r * quads + b
                weight[n, m] = place(heavy, b)
                value = place(rate, b)
                decay[n, m] = value
                power[n, m] = jnp.exp(-value)
                power_block[n, m] = jnp.exp(-float(BLOCK) * value)
        skip[m] = place(pick(2 * half), 0)

    def patch(m):
        halo_copy(m).wait_recv()
        for t in range(2):
            featured = []
            for j in range(3):
                rows = [
                    jnp.where(mine > 0, halo[m, 2 * j], 0.0),
                    jnp.where(mine > 0, halo[m, 2 * j + 1], 0.0),
                    head[m, 2 * j],
                    head[m, 2 * j + 1],
                ]
                featured.append(
                    filt[3 * j, m] * rows[t + 2]
                    + filt[3 * j + 1, m] * rows[t + 1]
                    + filt[3 * j + 2, m] * rows[t]
                )
            queries[m, t * ROWS : (t + 1) * ROWS, :] = featured[0]
            gated[m, t * ROWS : (t + 1) * ROWS, :] = featured[1] * featured[2]

    def feature(m):
        for j in range(3):
            fetch(j, m).wait()
        coefs = [[filt[3 * j + s, m] for s in range(3)] for j in range(3)]

        def step(b, olds):
            for j in range(3):
                rows = xb[j, pl.ds(pl.multiple_of(b * PAIR, PAIR), PAIR), m * WIDE : (m + 1) * WIDE]
                rows = rows.astype(F32)
                for h in range(PAIR // ROWS):
                    for i in range(ROWS):
                        at = (h * ROWS + i) * ROWS
                        tiles[j, at : at + ROWS, :] = rows[
                            h * ROWS : (h + 1) * ROWS, i * LANES : (i + 1) * LANES
                        ]
            olds = list(olds)
            for t in range(PAIR):
                featured = []
                for j in range(3):
                    now = tiles[j, token(t), :]
                    older, old = olds[2 * j], olds[2 * j + 1]
                    featured.append(coefs[j][0] * now + coefs[j][1] * old + coefs[j][2] * older)
                    olds[2 * j], olds[2 * j + 1] = old, now
                place = pl.ds(pl.multiple_of((b * PAIR + t) * ROWS, ROWS), ROWS)
                queries[m, place, :] = featured[0]
                gated[m, place, :] = featured[1] * featured[2]
            return tuple(olds)

        zero = jnp.zeros((ROWS, LANES), F32)
        olds = lax.fori_loop(0, length // PAIR, step, (zero,) * 6)
        for i in range(6):
            last[m, i] = olds[i]
        halo_copy(m).start()
        for j in range(3):
            rows = xb[j, 0:PAIR, m * WIDE : (m + 1) * WIDE].astype(F32)[:ROWS]
            for i in range(ROWS):
                tiles[j, i * ROWS : (i + 1) * ROWS, :] = rows[:, i * LANES : (i + 1) * LANES]
            for t in range(2):
                head[m, 2 * j + t] = tiles[j, token(t), :]

    def gather_states(m):
        def step(b, states):
            values = [
                gated[m, pl.ds(pl.multiple_of((b * BLOCK + i) * ROWS, ROWS), ROWS), :]
                for i in range(BLOCK)
            ]
            results = []
            for n in range(modes):
                rate = power[n, m]
                end = values[0]
                for i in range(1, BLOCK):
                    end = rate * end + values[i]
                end = weight[n, m] * end
                ends[m, b, n] = end
                results.append(power_block[n, m] * states[n] + end)
            return tuple(results)

        zero = jnp.zeros((ROWS, LANES), F32)
        states = lax.fori_loop(0, length // BLOCK, step, (zero,) * modes)
        for n in range(modes):
            state[m, n] = states[n]

    def state_copy(m, off):
        peer = lax.rem(my_seq + off, n_seq)
        return pltpu.make_async_remote_copy(
            src_ref=state.at[m, peer],
            dst_ref=got_state.at[m, my_seq],
            send_sem=send_state.at[m],
            recv_sem=recv_state.at[m],
            device_id=(my_chan, peer),
            device_id_type=MESH,
        )

    def total_copy(m, off):
        peer = lax.rem(my_chan + off, n_chan)
        return pltpu.make_async_remote_copy(
            src_ref=total.at[m],
            dst_ref=got_total.at[m, my_chan],
            send_sem=send_total.at[m],
            recv_sem=recv_total.at[m],
            device_id=(peer, my_seq),
            device_id_type=MESH,
        )

    def back_copy(m, off):
        peer = lax.rem(my_seq + off, n_seq)
        return pltpu.make_async_remote_copy(
            src_ref=back.at[m, peer],
            dst_ref=carried.at[m, my_seq],
            send_sem=send_back.at[m],
            recv_sem=recv_back.at[m],
            device_id=(my_chan, peer),
            device_id_type=MESH,
        )

    def wait_bytes(ref, count, m, sem):
        some = ref.at[m, pl.ds(0, count)]
        pltpu.make_async_copy(some, some, sem.at[m]).wait()

    def send_states(m):
        for off in range(1, n_seq):
            state_copy(m, off).start()
        got_state[m, my_seq] = state[m, my_seq]

    def scan_group(m):
        wait_bytes(got_state, n_seq - 1, m, recv_state)
        shrink = jnp.exp(-float(length) * decay[my_seq, m])
        running = jnp.zeros((ROWS, LANES), F32)
        for k in range(n_seq):
            before[m, k] = running
            running = shrink * running + got_state[m, k]
        total[m] = running
        for off in range(1, n_chan):
            total_copy(m, off).start()

    def scan_all(m):
        wait_bytes(got_total, n_chan - 1, m, recv_total)
        rate = decay[my_seq, m]
        shrink = jnp.exp(-float(length) * rate)
        shrink_group = jnp.exp(-float(length * n_seq) * rate)
        running = jnp.zeros((ROWS, LANES), F32)
        for c in range(n_chan - 1):
            running = jnp.where(c < my_chan, shrink_group * running + got_total[m, c], running)
        for k in range(n_seq):
            back[m, k] = before[m, k] + running
            running = shrink * running
        for off in range(1, n_seq):
            back_copy(m, off).start()
        carried[m, my_seq] = back[m, my_seq]

    def write(m):
        columns = pl.ds(m * WIDE, WIDE)
        return pltpu.make_async_copy(out_rows.at[:, columns], out_hbm.at[:, columns], out_sem.at[m])

    def convolve(m):
        wait_bytes(carried, n_seq - 1, m, recv_back)
        term = [weight[n, m] for n in range(modes)]
        for i in range(BLOCK):
            tap = term[0]
            for n in range(1, modes):
                tap = tap + term[n]
            taps[i] = tap + skip[m] if i == 0 else tap
            if i < BLOCK - 1:
                term = [term[n] * power[n, m] for n in range(modes)]

        def step(pair, states):
            for half in range(PAIR // BLOCK):
                b = pair * (PAIR // BLOCK) + half
                places = [
                    pl.ds(pl.multiple_of((b * BLOCK + i) * ROWS, ROWS), ROWS) for i in range(BLOCK)
                ]
                values = [gated[m, places[i], :] for i in range(BLOCK)]
                sums = []
                for i in range(BLOCK):
                    one = taps[0] * values[i]
                    for j in range(1, i + 1):
                        one = one + taps[j] * values[i - j]
                    sums.append(one)
                results = []
                for n in range(modes):
                    rate = power[n, m]
                    now = states[n]
                    for i in range(BLOCK):
                        now = now * rate
                        sums[i] = sums[i] + now
                    results.append(now + ends[m, b, n])
                states = tuple(results)
                for i in range(BLOCK):
                    out_tiles[token(half * BLOCK + i), :] = sums[i] * queries[m, places[i], :]
            for i in range(ROWS):
                parts = [
                    out_tiles[(h * ROWS + i) * ROWS : (h * ROWS + i + 1) * ROWS, :]
                    for h in range(PAIR // ROWS)
                ]
                lanes = m * WIDE + i * LANES
                out_rows[pl.ds(pl.multiple_of(pair * PAIR, PAIR), PAIR), lanes : lanes + LANES] = (
                    jnp.concatenate(parts, axis=0).astype(out_rows.dtype)
                )
            return states

        lax.fori_loop(0, length // PAIR, step, tuple(carried[m, n] for n in range(modes)))
        write(m).start()

    pl.semaphore_wait(barrier, signals)
    for off in range(1, chips):
        near_copy(off).start()
    for m in range(groups):
        feature(m)
    wait_near(recv_near)
    for m in range(groups):
        far_copy(m).start()
    for m in range(groups):
        patch(m)
        spread_params(m)
        gather_states(m)
        send_states(m)
    scan_group(0)
    for m in range(1, groups):
        scan_group(m)
        if m >= 2:
            scan_all(m - 2)
    scan_all(groups - 2)
    scan_all(groups - 1)
    for m in range(groups):
        convolve(m)
    wait_near(send_near)
    for m in range(groups):
        write(m).wait()
        halo_copy(m).wait_send()
        far_copy(m).wait_send()
        wait_bytes(got_state, n_seq - 1, m, send_state)
        wait_bytes(got_total, n_chan - 1, m, send_total)
        wait_bytes(carried, n_seq - 1, m, send_back)


def shards(n_chan, n_seq, projected, short_filter, residues, decays, skip):
    _, length, width = projected.shape
    modes = residues.shape[0]
    groups = width // WIDE
    hbm = pl.BlockSpec(memory_space=pltpu.HBM)
    dma = pltpu.SemaphoreType.DMA
    blocks = length // BLOCK
    return pl.pallas_call(
        functools.partial(kernel, n_chan, n_seq),
        out_shape=jax.ShapeDtypeStruct((length, width), projected.dtype),
        in_specs=[hbm] * 5,
        out_specs=pl.BlockSpec(memory_space=pl.ANY),
        scratch_shapes=[
            pltpu.VMEM((3, length, width), projected.dtype),
            pltpu.VMEM(short_filter.shape, F32),
            pltpu.VMEM((9, groups, ROWS, LANES), F32),
            pltpu.VMEM(residues.shape, F32),
            pltpu.VMEM(decays.shape, F32),
            pltpu.VMEM((1, skip.shape[0]), F32),
            pltpu.VMEM((3, PAIR * ROWS, LANES), F32),
            pltpu.VMEM((groups, length * ROWS, LANES), F32),
            pltpu.VMEM((groups, length * ROWS, LANES), F32),
            pltpu.VMEM((groups, blocks, modes, ROWS, LANES), F32),
            pltpu.VMEM((n_chan * n_seq // 2, 2, 2 * ROWS, LANES), F32),
            pltpu.VMEM((modes, groups, ROWS, LANES), F32),
            pltpu.VMEM((modes, groups, ROWS, LANES), F32),
            pltpu.VMEM((groups, ROWS, LANES), F32),
            pltpu.VMEM((groups, 6, ROWS, LANES), F32),
            pltpu.VMEM((groups, 6, ROWS, LANES), F32),
            pltpu.VMEM((groups, 6, ROWS, LANES), F32),
            pltpu.VMEM((modes, groups, ROWS, LANES), F32),
            pltpu.VMEM((modes, groups, ROWS, LANES), F32),
            pltpu.VMEM((BLOCK, ROWS, LANES), F32),
            pltpu.VMEM((groups, modes, ROWS, LANES), F32),
            pltpu.VMEM((groups, n_seq, ROWS, LANES), F32),
            pltpu.VMEM((groups, n_seq, ROWS, LANES), F32),
            pltpu.VMEM((groups, ROWS, LANES), F32),
            pltpu.VMEM((groups, n_chan, ROWS, LANES), F32),
            pltpu.VMEM((groups, n_seq, ROWS, LANES), F32),
            pltpu.VMEM((groups, modes, ROWS, LANES), F32),
            pltpu.VMEM((PAIR * ROWS, LANES), F32),
            pltpu.VMEM((length, width), projected.dtype),
            dma((groups, 3)),
            dma((4,)),
            dma((groups,)),
            dma,
            dma,
            dma((groups,)),
            dma((groups,)),
            dma((groups,)),
            dma((groups,)),
            dma((groups,)),
            dma((groups,)),
            dma((groups,)),
            dma((groups,)),
            dma((groups,)),
            dma((groups,)),
        ],
        compiler_params=pltpu.CompilerParams(
            collective_id=0, has_side_effects=True, vmem_limit_bytes=48 * 1024 * 1024
        ),
        name="hyena",
    )(projected, *[pltpu.with_memory_space_constraint(v, pltpu.HBM) for v in (short_filter, residues, decays, skip[None])])


def solution(mesh):
    return jax.shard_map(
        functools.partial(shards, mesh.shape["chan"], mesh.shape["seq"]),
        mesh=mesh,
        in_specs=(
            P(None, ("chan", "seq"), None),
            P(),
            P(None, ("chan", "seq")),
            P(None, ("chan", "seq")),
            P(("chan", "seq")),
        ),
        out_specs=P(("chan", "seq"), None),
        check_vma=False,
    )
```

```python
import functools

import jax
import jax.numpy as jnp
from jax import lax
from jax.experimental import pallas as pl
from jax.experimental.pallas import tpu as pltpu
from jax.sharding import PartitionSpec as P

LANES = 128
ROWS = 8
WIDE = LANES * ROWS
BLOCK = 8
PAIR = 16
MESH = pl.DeviceIdType.MESH
F32 = jnp.float32


SIDE = 4


def hops(*steps):
    return sum(min(step, SIDE - step) for step in steps)


CHIPS = sorted(
    [(dy, dx, dz) for dy in range(SIDE) for dx in range(SIDE) for dz in range(SIDE)][1:],
    key=lambda steps: -hops(*steps),
)
NEAR = sorted(
    [(dy, dz, dk) for dy in (0, SIDE // 2) for dz in range(SIDE) for dk in range(2)][1:],
    key=lambda steps: -hops(*steps[:2]) - steps[2] / 2,
)
ACROSS = sorted(
    [(dy, dx) for dy in range(2) for dx in range(SIDE)][1:],
    key=lambda steps: -steps[0] - hops(steps[1]),
)


def token(t):
    return pl.ds((t // ROWS) * ROWS * ROWS + t % ROWS, ROWS, stride=ROWS)


def kernel(
    n_chan,
    n_seq,
    x_hbm,
    filt_hbm,
    residues_hbm,
    rates_hbm,
    direct_hbm,
    out_hbm,
    xb,
    filt_rows,
    filt,
    residues,
    rates,
    direct,
    tiles,
    gated,
    queries,
    ends,
    params,
    weight,
    decay,
    skip,
    last,
    halo,
    head,
    power,
    power_block,
    state,
    got_state,
    before,
    total,
    got_total,
    back,
    carried,
    out_tiles,
    out_rows,
    in_sem,
    small_sem,
    out_sem,
    send_near,
    recv_near,
    send_far,
    recv_far,
    send_halo,
    recv_halo,
    send_state,
    recv_state,
    send_total,
    recv_total,
    send_back,
    recv_back,
):
    groups = gated.shape[0]
    length = x_hbm.shape[1]
    modes = weight.shape[0]
    my_chan = lax.axis_index("chan")
    my_seq = lax.axis_index("seq")
    count = n_chan * n_seq
    mine = my_chan * n_seq + my_seq
    after = lax.rem(mine + 1, count)
    ahead = lax.rem(mine + count - 1, count)
    chips = count // 2
    my_chip = mine // 2
    my_core = mine % 2
    other = 1 - my_core
    near = n_seq
    across = n_chan
    own = modes // near
    my_near = my_seq
    my_across = my_chan
    plane = 2 * SIDE
    my_z = my_seq % plane // 2
    my_y = my_seq // plane * 2 + my_chan // SIDE
    my_x = my_chan % SIDE
    places_z = [lax.rem(my_z + d, SIDE) * 2 for d in range(SIDE)]
    places_x = [lax.rem(my_x + d, SIDE) for d in range(SIDE)]
    turned_y = [lax.rem(my_y + d, SIDE) for d in range(SIDE)]
    chan_y = [y % 2 * SIDE for y in turned_y]
    seq_y = [y // 2 * plane for y in turned_y]
    cores = [my_core, other]
    half_y = my_chan // SIDE
    paired = [half_y * SIDE, (1 - half_y) * SIDE]

    def device(dy=0, dx=0, dz=0, dk=0):
        return (chan_y[dy] + places_x[dx], seq_y[dy] + places_z[dz] + cores[dk])

    barrier = pltpu.get_barrier_semaphore()

    def signal(target):
        pl.semaphore_signal(barrier, inc=1, device_id=target, device_id_type=MESH)

    for steps in CHIPS:
        signal(device(*steps))
    crossing = [(dy, dz) for dy, dz, dk in NEAR if dk]
    for dy, dz in crossing:
        signal(device(dy=dy, dz=dz, dk=1))
    signal((ahead // n_seq, ahead % n_seq))
    signals = len(CHIPS) + len(crossing) + 1

    def fetch(j, m):
        columns = pl.ds(m * WIDE, WIDE)
        return pltpu.make_async_copy(
            x_hbm.at[j, :, columns], xb.at[j, :, columns], in_sem.at[m, j]
        )

    small = [
        pltpu.make_async_copy(source, place, small_sem.at[i])
        for i, (source, place) in enumerate(
            [
                (residues_hbm, residues),
                (rates_hbm, rates),
                (direct_hbm, direct),
                (filt_hbm, filt_rows),
            ]
        )
    ]
    for copy in small:
        copy.start()
    for m in range(groups):
        for j in range(3):
            fetch(j, m).start()

    for copy in small:
        copy.wait()
    for j in range(3):
        for tap in range(3):
            for m in range(groups):
                for i in range(ROWS):
                    lanes = slice(m * WIDE + i * LANES, m * WIDE + (i + 1) * LANES)
                    filt[3 * j + tap, m, i : i + 1, :] = filt_rows[j, tap : tap + 1, lanes]

    part = residues.shape[1]
    quads = LANES // part
    half = modes // quads
    for r in range(half):
        for b in range(quads):
            n = r * quads + b
            lanes = slice(b * part, (b + 1) * part)
            params[my_core, my_chip, r, :, lanes] = residues[n : n + 1, :] * jnp.sqrt(rates[n : n + 1, :])
            params[my_core, my_chip, half + r, :, lanes] = rates[n : n + 1, :]
    params[my_core, my_chip, 2 * half, :, 0:part] = direct[...]
    params[my_core, my_chip, 2 * half, :, part:] = jnp.zeros((1, LANES - part), F32)

    def near_copy(steps):
        place = params.at[my_core, my_chip]
        return pltpu.make_async_remote_copy(
            src_ref=place,
            dst_ref=place,
            send_sem=send_near,
            recv_sem=recv_near,
            device_id=device(*steps),
            device_id_type=MESH,
        )

    def wait_near(sem):
        some = params.at[0, pl.ds(0, chips - 1)]
        pltpu.make_async_copy(some, some, sem).wait()

    def far_copy(m):
        place = params.at[my_core, pl.ds(m * (chips // groups), chips // groups)]
        return pltpu.make_async_remote_copy(
            src_ref=place,
            dst_ref=place,
            send_sem=send_far.at[m],
            recv_sem=recv_far.at[m],
            device_id=device(dk=1),
            device_id_type=MESH,
        )

    def halo_copy(m):
        return pltpu.make_async_remote_copy(
            src_ref=last.at[m],
            dst_ref=halo.at[m],
            send_sem=send_halo.at[m],
            recv_sem=recv_halo.at[m],
            device_id=(after // n_seq, after % n_seq),
            device_id_type=MESH,
        )

    def spread_params(m):
        far_copy(m).wait_recv()
        group = lax.broadcasted_iota(jnp.int32, (ROWS, LANES), 1) // part

        def pick(row):
            found = []
            for i in range(quads):
                found.append(
                    jnp.concatenate(
                        [
                            params[i % 2, ((m * ROWS + j) * quads + i) // 2, row, :, :]
                            for j in range(ROWS)
                        ],
                        axis=0,
                    )
                )
            return found

        def place(found, b):
            value = None
            for i in range(quads):
                shift = (i - b) % quads * part
                turned = pltpu.roll(found[i], shift, 1) if shift else found[i]
                value = turned if i == 0 else jnp.where(group == i, turned, value)
            return value

        for r in range(half):
            heavy = pick(r)
            rate = pick(half + r)
            for b in range(quads):
                n = r * quads + b
                weight[n, m] = place(heavy, b)
                value = place(rate, b)
                decay[n, m] = value
                power[n, m] = jnp.exp(-value)
                power_block[n, m] = jnp.exp(-float(BLOCK) * value)
        skip[m] = place(pick(2 * half), 0)

    def patch(m):
        halo_copy(m).wait_recv()
        for t in range(2):
            featured = []
            for j in range(3):
                rows = [
                    jnp.where(mine > 0, halo[m, 2 * j], 0.0),
                    jnp.where(mine > 0, halo[m, 2 * j + 1], 0.0),
                    head[m, 2 * j],
                    head[m, 2 * j + 1],
                ]
                featured.append(
                    filt[3 * j, m] * rows[t + 2]
                    + filt[3 * j + 1, m] * rows[t + 1]
                    + filt[3 * j + 2, m] * rows[t]
                )
            queries[m, t * ROWS : (t + 1) * ROWS, :] = featured[0]
            gated[m, t * ROWS : (t + 1) * ROWS, :] = featured[1] * featured[2]

    def feature(m):
        for j in range(3):
            fetch(j, m).wait()
        coefs = [[filt[3 * j + s, m] for s in range(3)] for j in range(3)]

        def step(b, olds):
            for j in range(3):
                rows = xb[j, pl.ds(pl.multiple_of(b * PAIR, PAIR), PAIR), m * WIDE : (m + 1) * WIDE]
                rows = rows.astype(F32)
                for h in range(PAIR // ROWS):
                    for i in range(ROWS):
                        at = (h * ROWS + i) * ROWS
                        tiles[j, at : at + ROWS, :] = rows[
                            h * ROWS : (h + 1) * ROWS, i * LANES : (i + 1) * LANES
                        ]
            olds = list(olds)
            for t in range(PAIR):
                featured = []
                for j in range(3):
                    now = tiles[j, token(t), :]
                    older, old = olds[2 * j], olds[2 * j + 1]
                    featured.append(coefs[j][0] * now + coefs[j][1] * old + coefs[j][2] * older)
                    olds[2 * j], olds[2 * j + 1] = old, now
                place = pl.ds(pl.multiple_of((b * PAIR + t) * ROWS, ROWS), ROWS)
                queries[m, place, :] = featured[0]
                gated[m, place, :] = featured[1] * featured[2]
            return tuple(olds)

        zero = jnp.zeros((ROWS, LANES), F32)
        olds = lax.fori_loop(0, length // PAIR, step, (zero,) * 6)
        for i in range(6):
            last[m, i] = olds[i]
        halo_copy(m).start()
        for j in range(3):
            rows = xb[j, 0:PAIR, m * WIDE : (m + 1) * WIDE].astype(F32)[:ROWS]
            for i in range(ROWS):
                tiles[j, i * ROWS : (i + 1) * ROWS, :] = rows[:, i * LANES : (i + 1) * LANES]
            for t in range(2):
                head[m, 2 * j + t] = tiles[j, token(t), :]

    def gather_states(m):
        some = modes // 2
        for part in range(0, modes, some):
            chosen = range(part, part + some)
            rate = [power[n, m] for n in chosen]
            rate_block = [power_block[n, m] for n in chosen]
            heavy = [weight[n, m] for n in chosen]

            def step(pair, states):
                for half in range(PAIR // BLOCK):
                    b = pair * (PAIR // BLOCK) + half
                    values = [
                        gated[m, pl.ds(pl.multiple_of((b * BLOCK + i) * ROWS, ROWS), ROWS), :]
                        for i in range(BLOCK)
                    ]
                    results = []
                    for k, n in enumerate(chosen):
                        end = values[0]
                        for i in range(1, BLOCK):
                            end = rate[k] * end + values[i]
                        end = heavy[k] * end
                        ends[m, b, n] = end
                        results.append(rate_block[k] * states[k] + end)
                    states = tuple(results)
                return states

            zero = jnp.zeros((ROWS, LANES), F32)
            states = lax.fori_loop(0, length // PAIR, step, (zero,) * some)
            for k, n in enumerate(chosen):
                state[m, n // own, n % own] = states[k]

    def state_copy(m, steps):
        dy, dz, dk = steps
        target = device(dy=dy, dz=dz, dk=dk)
        peer = target[1]
        return pltpu.make_async_remote_copy(
            src_ref=state.at[m, peer],
            dst_ref=got_state.at[m, my_near],
            send_sem=send_state.at[m],
            recv_sem=recv_state.at[m],
            device_id=target,
            device_id_type=MESH,
        )

    def total_copy(m, steps):
        return pltpu.make_async_remote_copy(
            src_ref=total.at[m],
            dst_ref=got_total.at[m, my_across],
            send_sem=send_total.at[m],
            recv_sem=recv_total.at[m],
            device_id=(paired[steps[0]] + places_x[steps[1]], my_seq),
            device_id_type=MESH,
        )

    def back_copy(m, steps):
        dy, dz, dk = steps
        target = device(dy=dy, dz=dz, dk=dk)
        peer = target[1]
        return pltpu.make_async_remote_copy(
            src_ref=back.at[m, peer],
            dst_ref=carried.at[m, my_near],
            send_sem=send_back.at[m],
            recv_sem=recv_back.at[m],
            device_id=target,
            device_id_type=MESH,
        )

    def wait_bytes(ref, count, m, sem):
        some = ref.at[m, pl.ds(0, count)]
        pltpu.make_async_copy(some, some, sem.at[m]).wait()

    def send_states(m):
        for steps in NEAR:
            state_copy(m, steps).start()
        got_state[m, my_near] = state[m, my_near]

    def scan_group(m):
        wait_bytes(got_state, near - 1, m, recv_state)
        for u in range(own):
            shrink = jnp.exp(-float(length) * decay[my_near * own + u, m])
            running = jnp.zeros((ROWS, LANES), F32)
            for k in range(near):
                before[m, k, u] = running
                running = shrink * running + got_state[m, k, u]
            total[m, u] = running
        for steps in ACROSS:
            total_copy(m, steps).start()

    def scan_all(m):
        wait_bytes(got_total, across - 1, m, recv_total)
        for u in range(own):
            rate = decay[my_near * own + u, m]
            shrink = jnp.exp(-float(length) * rate)
            shrink_group = jnp.exp(-float(length * near) * rate)
            running = jnp.zeros((ROWS, LANES), F32)
            for c in range(across - 1):
                running = jnp.where(
                    c < my_across, shrink_group * running + got_total[m, c, u], running
                )
            for k in range(near):
                back[m, k, u] = before[m, k, u] + running
                running = shrink * running
        for steps in NEAR:
            back_copy(m, steps).start()
        carried[m, my_near] = back[m, my_near]

    def write(m):
        columns = pl.ds(m * WIDE, WIDE)
        return pltpu.make_async_copy(out_rows.at[:, columns], out_hbm.at[:, columns], out_sem.at[m])

    def block_places(b):
        return [pl.ds(pl.multiple_of((b * BLOCK + i) * ROWS, ROWS), ROWS) for i in range(BLOCK)]

    def convolve_block(m):
        term = [weight[n, m] for n in range(modes)]
        taps = []
        for i in range(BLOCK):
            tap = term[0]
            for n in range(1, modes):
                tap = tap + term[n]
            taps.append(tap + skip[m] if i == 0 else tap)
            if i < BLOCK - 1:
                term = [term[n] * power[n, m] for n in range(modes)]

        def step(pair, _):
            for half in range(PAIR // BLOCK):
                places = block_places(pair * (PAIR // BLOCK) + half)
                values = [gated[m, places[i], :] for i in range(BLOCK)]
                for i in range(BLOCK):
                    one = taps[0] * values[i]
                    for j in range(1, i + 1):
                        one = one + taps[j] * values[i - j]
                    gated[m, places[i], :] = one
            return 0

        lax.fori_loop(0, length // PAIR, step, 0)

    def convolve(m):
        wait_bytes(carried, near - 1, m, recv_back)

        def step(pair, states):
            for half in range(PAIR // BLOCK):
                b = pair * (PAIR // BLOCK) + half
                places = block_places(b)
                sums = [gated[m, places[i], :] for i in range(BLOCK)]
                results = []
                for n in range(modes):
                    rate = power[n, m]
                    now = states[n]
                    for i in range(BLOCK):
                        now = now * rate
                        sums[i] = sums[i] + now
                    results.append(now + ends[m, b, n])
                states = tuple(results)
                for i in range(BLOCK):
                    out_tiles[token(half * BLOCK + i), :] = sums[i] * queries[m, places[i], :]
            for i in range(ROWS):
                parts = [
                    out_tiles[(h * ROWS + i) * ROWS : (h * ROWS + i + 1) * ROWS, :]
                    for h in range(PAIR // ROWS)
                ]
                lanes = m * WIDE + i * LANES
                out_rows[pl.ds(pl.multiple_of(pair * PAIR, PAIR), PAIR), lanes : lanes + LANES] = (
                    jnp.concatenate(parts, axis=0).astype(out_rows.dtype)
                )
            return states

        lax.fori_loop(0, length // PAIR, step, tuple(carried[m, n // own, n % own] for n in range(modes)))
        write(m).start()

    pl.semaphore_wait(barrier, signals)
    for steps in CHIPS:
        near_copy(steps).start()
    for m in range(groups):
        feature(m)
    wait_near(recv_near)
    for m in range(groups):
        far_copy(m).start()
    def first(m):
        patch(m)
        spread_params(m)
        gather_states(m)
        send_states(m)

    steps = [(first, 0), (first, 1), (first, 2), (first, 3)]
    steps += [(scan_group, 0), (convolve_block, 0), (scan_group, 1), (convolve_block, 1)]
    steps += [(scan_group, 2), (convolve_block, 2), (scan_all, 0), (scan_group, 3)]
    steps += [(convolve_block, 3), (scan_all, 1), (scan_all, 2), (scan_all, 3)]
    steps += [(convolve, 0), (convolve, 1), (convolve, 2), (convolve, 3)]
    for act, m in steps:
        act(m)
    wait_near(send_near)
    for m in range(groups):
        write(m).wait()
        halo_copy(m).wait_send()
        far_copy(m).wait_send()
        wait_bytes(got_state, near - 1, m, send_state)
        wait_bytes(got_total, across - 1, m, send_total)
        wait_bytes(carried, near - 1, m, send_back)


def shards(n_chan, n_seq, projected, short_filter, residues, decays, skip):
    _, length, width = projected.shape
    modes = residues.shape[0]
    groups = width // WIDE
    hbm = pl.BlockSpec(memory_space=pltpu.HBM)
    dma = pltpu.SemaphoreType.DMA
    blocks = length // BLOCK
    near = n_seq
    own = modes // near
    rows = 2 * modes * residues.shape[1] // LANES + 1
    return pl.pallas_call(
        functools.partial(kernel, n_chan, n_seq),
        out_shape=jax.ShapeDtypeStruct((length, width), projected.dtype),
        in_specs=[hbm] * 5,
        out_specs=pl.BlockSpec(memory_space=pl.ANY),
        scratch_shapes=[
            pltpu.VMEM((3, length, width), projected.dtype),
            pltpu.VMEM(short_filter.shape, F32),
            pltpu.VMEM((9, groups, ROWS, LANES), F32),
            pltpu.VMEM(residues.shape, F32),
            pltpu.VMEM(decays.shape, F32),
            pltpu.VMEM((1, skip.shape[0]), F32),
            pltpu.VMEM((3, PAIR * ROWS, LANES), F32),
            pltpu.VMEM((groups, length * ROWS, LANES), F32),
            pltpu.VMEM((groups, length * ROWS, LANES), F32),
            pltpu.VMEM((groups, blocks, modes, ROWS, LANES), F32),
            pltpu.VMEM((2, n_chan * n_seq // 2, rows, 1, LANES), F32),
            pltpu.VMEM((modes, groups, ROWS, LANES), F32),
            pltpu.VMEM((modes, groups, ROWS, LANES), F32),
            pltpu.VMEM((groups, ROWS, LANES), F32),
            pltpu.VMEM((groups, 6, ROWS, LANES), F32),
            pltpu.VMEM((groups, 6, ROWS, LANES), F32),
            pltpu.VMEM((groups, 6, ROWS, LANES), F32),
            pltpu.VMEM((modes, groups, ROWS, LANES), F32),
            pltpu.VMEM((modes, groups, ROWS, LANES), F32),
            pltpu.VMEM((groups, near, own, ROWS, LANES), F32),
            pltpu.VMEM((groups, near, own, ROWS, LANES), F32),
            pltpu.VMEM((groups, near, own, ROWS, LANES), F32),
            pltpu.VMEM((groups, own, ROWS, LANES), F32),
            pltpu.VMEM((groups, n_chan * n_seq // near, own, ROWS, LANES), F32),
            pltpu.VMEM((groups, near, own, ROWS, LANES), F32),
            pltpu.VMEM((groups, near, own, ROWS, LANES), F32),
            pltpu.VMEM((PAIR * ROWS, LANES), F32),
            pltpu.VMEM((length, width), projected.dtype),
            dma((groups, 3)),
            dma((4,)),
            dma((groups,)),
            dma,
            dma,
            dma((groups,)),
            dma((groups,)),
            dma((groups,)),
            dma((groups,)),
            dma((groups,)),
            dma((groups,)),
            dma((groups,)),
            dma((groups,)),
            dma((groups,)),
            dma((groups,)),
        ],
        compiler_params=pltpu.CompilerParams(
            collective_id=0, has_side_effects=True, vmem_limit_bytes=48 * 1024 * 1024
        ),
        name="hyena",
    )(projected, *[pltpu.with_memory_space_constraint(v, pltpu.HBM) for v in (short_filter, residues, decays, skip[None])])


def solution(mesh):
    return jax.shard_map(
        functools.partial(shards, mesh.shape["chan"], mesh.shape["seq"]),
        mesh=mesh,
        in_specs=(
            P(None, ("chan", "seq"), None),
            P(),
            P(None, ("chan", "seq")),
            P(None, ("chan", "seq")),
            P(("chan", "seq")),
        ),
        out_specs=P(("chan", "seq"), None),
        check_vma=False,
    )
```

```python
import functools

import jax
import jax.numpy as jnp
from jax import lax
from jax.experimental import pallas as pl
from jax.experimental.pallas import tpu as pltpu
from jax.sharding import PartitionSpec as P

LANES = 128
ROWS = 8
WIDE = LANES * ROWS
BLOCK = 8
PAIR = 16
MESH = pl.DeviceIdType.MESH
F32 = jnp.float32


SIDE = 4


def hops(*steps):
    return sum(min(step, SIDE - step) for step in steps)


CHIPS = sorted(
    [(dy, dx, dz) for dy in range(SIDE) for dx in range(SIDE) for dz in range(SIDE)][1:],
    key=lambda steps: -hops(*steps),
)
NEAR = sorted(
    [(dz, dk) for dz in range(SIDE) for dk in range(2)][1:],
    key=lambda steps: -hops(steps[0]) - steps[1] / 2,
)
ACROSS = sorted(
    [(dy, dx) for dy in range(SIDE) for dx in range(SIDE)][1:], key=lambda steps: -hops(*steps)
)


def token(t):
    return pl.ds((t // ROWS) * ROWS * ROWS + t % ROWS, ROWS, stride=ROWS)


def kernel(
    n_chan,
    n_seq,
    x_hbm,
    filt_hbm,
    residues_hbm,
    rates_hbm,
    direct_hbm,
    out_hbm,
    xb,
    filt_rows,
    filt,
    residues,
    rates,
    direct,
    tiles,
    gated,
    queries,
    ends,
    params,
    weight,
    decay,
    skip,
    last,
    halo,
    head,
    power,
    power_block,
    state,
    got_state,
    before,
    total,
    got_total,
    back,
    carried,
    out_tiles,
    out_rows,
    in_sem,
    small_sem,
    out_sem,
    send_near,
    recv_near,
    send_far,
    recv_far,
    send_halo,
    recv_halo,
    send_state,
    recv_state,
    send_total,
    recv_total,
    send_back,
    recv_back,
):
    groups = gated.shape[0]
    length = x_hbm.shape[1]
    modes = weight.shape[0]
    my_chan = lax.axis_index("chan")
    my_seq = lax.axis_index("seq")
    count = n_chan * n_seq
    mine = my_chan * n_seq + my_seq
    after = lax.rem(mine + 1, count)
    ahead = lax.rem(mine + count - 1, count)
    chips = count // 2
    my_chip = mine // 2
    my_core = mine % 2
    other = 1 - my_core
    near = 2 * SIDE
    across = count // near
    own = modes // near
    my_near = mine % near
    my_across = mine // near
    plane = 2 * SIDE
    my_z = my_seq % plane // 2
    my_y = my_seq // plane * 2 + my_chan // SIDE
    my_x = my_chan % SIDE
    places_z = [lax.rem(my_z + d, SIDE) * 2 for d in range(SIDE)]
    places_x = [lax.rem(my_x + d, SIDE) for d in range(SIDE)]
    turned_y = [lax.rem(my_y + d, SIDE) for d in range(SIDE)]
    chan_y = [y % 2 * SIDE for y in turned_y]
    seq_y = [y // 2 * plane for y in turned_y]
    cores = [my_core, other]

    def device(dy=0, dx=0, dz=0, dk=0):
        return (chan_y[dy] + places_x[dx], seq_y[dy] + places_z[dz] + cores[dk])

    barrier = pltpu.get_barrier_semaphore()

    def signal(target):
        pl.semaphore_signal(barrier, inc=1, device_id=target, device_id_type=MESH)

    for steps in CHIPS:
        signal(device(*steps))
    crossing = [dz for dz, dk in NEAR if dk]
    for dz in crossing:
        signal(device(dz=dz, dk=1))
    signal((ahead // n_seq, ahead % n_seq))
    signals = len(CHIPS) + len(crossing) + 1

    def fetch(j, m):
        columns = pl.ds(m * WIDE, WIDE)
        return pltpu.make_async_copy(
            x_hbm.at[j, :, columns], xb.at[j, :, columns], in_sem.at[m, j]
        )

    small = [
        pltpu.make_async_copy(source, place, small_sem.at[i])
        for i, (source, place) in enumerate(
            [
                (residues_hbm, residues),
                (rates_hbm, rates),
                (direct_hbm, direct),
                (filt_hbm, filt_rows),
            ]
        )
    ]
    for copy in small:
        copy.start()
    for m in range(groups):
        for j in range(3):
            fetch(j, m).start()

    for copy in small:
        copy.wait()
    for j in range(3):
        for tap in range(3):
            for m in range(groups):
                for i in range(ROWS):
                    lanes = slice(m * WIDE + i * LANES, m * WIDE + (i + 1) * LANES)
                    filt[3 * j + tap, m, i : i + 1, :] = filt_rows[j, tap : tap + 1, lanes]

    part = residues.shape[1]
    quads = LANES // part
    half = modes // quads
    for r in range(half):
        for b in range(quads):
            n = r * quads + b
            lanes = slice(b * part, (b + 1) * part)
            params[my_core, my_chip, r, :, lanes] = residues[n : n + 1, :] * jnp.sqrt(rates[n : n + 1, :])
            params[my_core, my_chip, half + r, :, lanes] = rates[n : n + 1, :]
    params[my_core, my_chip, 2 * half, :, 0:part] = direct[...]
    params[my_core, my_chip, 2 * half, :, part:] = jnp.zeros((1, LANES - part), F32)

    def near_copy(steps):
        place = params.at[my_core, my_chip]
        return pltpu.make_async_remote_copy(
            src_ref=place,
            dst_ref=place,
            send_sem=send_near,
            recv_sem=recv_near,
            device_id=device(*steps),
            device_id_type=MESH,
        )

    def wait_near(sem):
        some = params.at[0, pl.ds(0, chips - 1)]
        pltpu.make_async_copy(some, some, sem).wait()

    def far_copy(m):
        place = params.at[my_core, pl.ds(m * (chips // groups), chips // groups)]
        return pltpu.make_async_remote_copy(
            src_ref=place,
            dst_ref=place,
            send_sem=send_far.at[m],
            recv_sem=recv_far.at[m],
            device_id=device(dk=1),
            device_id_type=MESH,
        )

    def halo_copy(m):
        return pltpu.make_async_remote_copy(
            src_ref=last.at[m],
            dst_ref=halo.at[m],
            send_sem=send_halo.at[m],
            recv_sem=recv_halo.at[m],
            device_id=(after // n_seq, after % n_seq),
            device_id_type=MESH,
        )

    def spread_params(m):
        far_copy(m).wait_recv()
        group = lax.broadcasted_iota(jnp.int32, (ROWS, LANES), 1) // part

        def pick(row):
            found = []
            for i in range(quads):
                found.append(
                    jnp.concatenate(
                        [
                            params[i % 2, ((m * ROWS + j) * quads + i) // 2, row, :, :]
                            for j in range(ROWS)
                        ],
                        axis=0,
                    )
                )
            return found

        def place(found, b):
            value = None
            for i in range(quads):
                shift = (i - b) % quads * part
                turned = pltpu.roll(found[i], shift, 1) if shift else found[i]
                value = turned if i == 0 else jnp.where(group == i, turned, value)
            return value

        for r in range(half):
            heavy = pick(r)
            rate = pick(half + r)
            for b in range(quads):
                n = r * quads + b
                weight[n, m] = place(heavy, b)
                value = place(rate, b)
                decay[n, m] = value
                power[n, m] = jnp.exp(-value)
                power_block[n, m] = jnp.exp(-float(BLOCK) * value)
        skip[m] = place(pick(2 * half), 0)

    def patch(m):
        halo_copy(m).wait_recv()
        for t in range(2):
            featured = []
            for j in range(3):
                rows = [
                    jnp.where(mine > 0, halo[m, 2 * j], 0.0),
                    jnp.where(mine > 0, halo[m, 2 * j + 1], 0.0),
                    head[m, 2 * j],
                    head[m, 2 * j + 1],
                ]
                featured.append(
                    filt[3 * j, m] * rows[t + 2]
                    + filt[3 * j + 1, m] * rows[t + 1]
                    + filt[3 * j + 2, m] * rows[t]
                )
            queries[m, t * ROWS : (t + 1) * ROWS, :] = featured[0]
            gated[m, t * ROWS : (t + 1) * ROWS, :] = featured[1] * featured[2]

    def feature(m):
        for j in range(3):
            fetch(j, m).wait()
        coefs = [[filt[3 * j + s, m] for s in range(3)] for j in range(3)]

        def step(b, olds):
            for j in range(3):
                rows = xb[j, pl.ds(pl.multiple_of(b * PAIR, PAIR), PAIR), m * WIDE : (m + 1) * WIDE]
                rows = rows.astype(F32)
                for h in range(PAIR // ROWS):
                    for i in range(ROWS):
                        at = (h * ROWS + i) * ROWS
                        tiles[j, at : at + ROWS, :] = rows[
                            h * ROWS : (h + 1) * ROWS, i * LANES : (i + 1) * LANES
                        ]
            olds = list(olds)
            for t in range(PAIR):
                featured = []
                for j in range(3):
                    now = tiles[j, token(t), :]
                    older, old = olds[2 * j], olds[2 * j + 1]
                    featured.append(coefs[j][0] * now + coefs[j][1] * old + coefs[j][2] * older)
                    olds[2 * j], olds[2 * j + 1] = old, now
                place = pl.ds(pl.multiple_of((b * PAIR + t) * ROWS, ROWS), ROWS)
                queries[m, place, :] = featured[0]
                gated[m, place, :] = featured[1] * featured[2]
            return tuple(olds)

        zero = jnp.zeros((ROWS, LANES), F32)
        olds = lax.fori_loop(0, length // PAIR, step, (zero,) * 6)
        for i in range(6):
            last[m, i] = olds[i]
        halo_copy(m).start()
        for j in range(3):
            rows = xb[j, 0:PAIR, m * WIDE : (m + 1) * WIDE].astype(F32)[:ROWS]
            for i in range(ROWS):
                tiles[j, i * ROWS : (i + 1) * ROWS, :] = rows[:, i * LANES : (i + 1) * LANES]
            for t in range(2):
                head[m, 2 * j + t] = tiles[j, token(t), :]

    def gather_states(m):
        some = modes // 2
        for part in range(0, modes, some):
            chosen = range(part, part + some)
            rate = [power[n, m] for n in chosen]
            rate_block = [power_block[n, m] for n in chosen]
            heavy = [weight[n, m] for n in chosen]

            def step(pair, states):
                for half in range(PAIR // BLOCK):
                    b = pair * (PAIR // BLOCK) + half
                    values = [
                        gated[m, pl.ds(pl.multiple_of((b * BLOCK + i) * ROWS, ROWS), ROWS), :]
                        for i in range(BLOCK)
                    ]
                    results = []
                    for k, n in enumerate(chosen):
                        end = values[0]
                        for i in range(1, BLOCK):
                            end = rate[k] * end + values[i]
                        end = heavy[k] * end
                        ends[m, b, n] = end
                        results.append(rate_block[k] * states[k] + end)
                    states = tuple(results)
                return states

            zero = jnp.zeros((ROWS, LANES), F32)
            states = lax.fori_loop(0, length // PAIR, step, (zero,) * some)
            for k, n in enumerate(chosen):
                state[m, n // own, n % own] = states[k]

    def state_copy(m, steps):
        dz, dk = steps
        target = device(dz=dz, dk=dk)
        peer = target[1] % near
        return pltpu.make_async_remote_copy(
            src_ref=state.at[m, peer],
            dst_ref=got_state.at[m, my_near],
            send_sem=send_state.at[m],
            recv_sem=recv_state.at[m],
            device_id=target,
            device_id_type=MESH,
        )

    def each_total(m, act):
        for i, steps in enumerate(ACROSS):
            target = device(*steps)
            copy = pltpu.make_async_remote_copy(
                src_ref=total.at[m],
                dst_ref=got_total.at[m, my_across],
                send_sem=send_total.at[m, i],
                recv_sem=recv_total.at[m, my_across],
                device_id=target,
                device_id_type=MESH,
            )

            @pl.when(target[0] * 2 + target[1] // near > my_across)
            def _():
                act(copy)

    def back_copy(m, steps):
        dz, dk = steps
        target = device(dz=dz, dk=dk)
        peer = target[1] % near
        return pltpu.make_async_remote_copy(
            src_ref=back.at[m, peer],
            dst_ref=carried.at[m, my_near],
            send_sem=send_back.at[m],
            recv_sem=recv_back.at[m],
            device_id=target,
            device_id_type=MESH,
        )

    def wait_bytes(ref, count, m, sem):
        some = ref.at[m, pl.ds(0, count)]
        pltpu.make_async_copy(some, some, sem.at[m]).wait()

    def send_states(m):
        for steps in NEAR:
            state_copy(m, steps).start()
        got_state[m, my_near] = state[m, my_near]

    def scan_group(m):
        wait_bytes(got_state, near - 1, m, recv_state)
        for u in range(own):
            shrink = jnp.exp(-float(length) * decay[my_near * own + u, m])
            running = jnp.zeros((ROWS, LANES), F32)
            for k in range(near):
                before[m, k, u] = running
                running = shrink * running + got_state[m, k, u]
            total[m, u] = running
        each_total(m, lambda copy: copy.start())

    def scan_all(m):
        for c in range(across - 1):
            place = got_total.at[m, c]
            arrival = pltpu.make_async_copy(place, place, recv_total.at[m, c])

            @pl.when(c < my_across)
            def _():
                arrival.wait()

        for u in range(own):
            rate = decay[my_near * own + u, m]
            shrink = jnp.exp(-float(length) * rate)
            shrink_group = jnp.exp(-float(length * near) * rate)
            running = jnp.zeros((ROWS, LANES), F32)
            for c in range(across - 1):
                running = jnp.where(
                    c < my_across, shrink_group * running + got_total[m, c, u], running
                )
            for k in range(near):
                back[m, k, u] = before[m, k, u] + running
                running = shrink * running
        for steps in NEAR:
            back_copy(m, steps).start()
        carried[m, my_near] = back[m, my_near]

    def write(m):
        columns = pl.ds(m * WIDE, WIDE)
        return pltpu.make_async_copy(out_rows.at[:, columns], out_hbm.at[:, columns], out_sem.at[m])

    def block_places(b):
        return [pl.ds(pl.multiple_of((b * BLOCK + i) * ROWS, ROWS), ROWS) for i in range(BLOCK)]

    def convolve_block(m):
        term = [weight[n, m] for n in range(modes)]
        taps = []
        for i in range(BLOCK):
            tap = term[0]
            for n in range(1, modes):
                tap = tap + term[n]
            taps.append(tap + skip[m] if i == 0 else tap)
            if i < BLOCK - 1:
                term = [term[n] * power[n, m] for n in range(modes)]

        def step(pair, _):
            for half in range(PAIR // BLOCK):
                places = block_places(pair * (PAIR // BLOCK) + half)
                values = [gated[m, places[i], :] for i in range(BLOCK)]
                for i in range(BLOCK):
                    one = taps[0] * values[i]
                    for j in range(1, i + 1):
                        one = one + taps[j] * values[i - j]
                    gated[m, places[i], :] = one
            return 0

        lax.fori_loop(0, length // PAIR, step, 0)

    def convolve(m):
        wait_bytes(carried, near - 1, m, recv_back)

        def step(pair, states):
            for half in range(PAIR // BLOCK):
                b = pair * (PAIR // BLOCK) + half
                places = block_places(b)
                sums = [gated[m, places[i], :] for i in range(BLOCK)]
                results = []
                for n in range(modes):
                    rate = power[n, m]
                    now = states[n]
                    for i in range(BLOCK):
                        now = now * rate
                        sums[i] = sums[i] + now
                    results.append(now + ends[m, b, n])
                states = tuple(results)
                for i in range(BLOCK):
                    out_tiles[token(half * BLOCK + i), :] = sums[i] * queries[m, places[i], :]
            for i in range(ROWS):
                parts = [
                    out_tiles[(h * ROWS + i) * ROWS : (h * ROWS + i + 1) * ROWS, :]
                    for h in range(PAIR // ROWS)
                ]
                lanes = m * WIDE + i * LANES
                out_rows[pl.ds(pl.multiple_of(pair * PAIR, PAIR), PAIR), lanes : lanes + LANES] = (
                    jnp.concatenate(parts, axis=0).astype(out_rows.dtype)
                )
            return states

        lax.fori_loop(0, length // PAIR, step, tuple(carried[m, n // own, n % own] for n in range(modes)))
        write(m).start()

    pl.semaphore_wait(barrier, signals)
    for steps in CHIPS:
        near_copy(steps).start()
    for m in range(groups):
        feature(m)
    wait_near(recv_near)
    for m in range(groups):
        far_copy(m).start()
    def first(m):
        patch(m)
        spread_params(m)
        gather_states(m)
        send_states(m)

    steps = [(first, 0), (first, 1), (first, 2), (scan_group, 0), (first, 3)]
    steps += [(scan_group, 1), (convolve_block, 0), (scan_group, 2), (convolve_block, 1)]
    steps += [(scan_all, 0), (scan_group, 3), (convolve_block, 2), (scan_all, 1)]
    steps += [(convolve_block, 3), (scan_all, 2), (scan_all, 3)]
    steps += [(convolve, 0), (convolve, 1), (convolve, 2), (convolve, 3)]
    for act, m in steps:
        act(m)
    wait_near(send_near)
    for m in range(groups):
        write(m).wait()
        halo_copy(m).wait_send()
        far_copy(m).wait_send()
        wait_bytes(got_state, near - 1, m, send_state)
        each_total(m, lambda copy: copy.wait_send())
        wait_bytes(carried, near - 1, m, send_back)


def shards(n_chan, n_seq, projected, short_filter, residues, decays, skip):
    _, length, width = projected.shape
    modes = residues.shape[0]
    groups = width // WIDE
    hbm = pl.BlockSpec(memory_space=pltpu.HBM)
    dma = pltpu.SemaphoreType.DMA
    blocks = length // BLOCK
    near = 2 * SIDE
    across = n_chan * n_seq // near
    own = modes // near
    rows = 2 * modes * residues.shape[1] // LANES + 1
    return pl.pallas_call(
        functools.partial(kernel, n_chan, n_seq),
        out_shape=jax.ShapeDtypeStruct((length, width), projected.dtype),
        in_specs=[hbm] * 5,
        out_specs=pl.BlockSpec(memory_space=pl.ANY),
        scratch_shapes=[
            pltpu.VMEM((3, length, width), projected.dtype),
            pltpu.VMEM(short_filter.shape, F32),
            pltpu.VMEM((9, groups, ROWS, LANES), F32),
            pltpu.VMEM(residues.shape, F32),
            pltpu.VMEM(decays.shape, F32),
            pltpu.VMEM((1, skip.shape[0]), F32),
            pltpu.VMEM((3, PAIR * ROWS, LANES), F32),
            pltpu.VMEM((groups, length * ROWS, LANES), F32),
            pltpu.VMEM((groups, length * ROWS, LANES), F32),
            pltpu.VMEM((groups, blocks, modes, ROWS, LANES), F32),
            pltpu.VMEM((2, n_chan * n_seq // 2, rows, 1, LANES), F32),
            pltpu.VMEM((modes, groups, ROWS, LANES), F32),
            pltpu.VMEM((modes, groups, ROWS, LANES), F32),
            pltpu.VMEM((groups, ROWS, LANES), F32),
            pltpu.VMEM((groups, 6, ROWS, LANES), F32),
            pltpu.VMEM((groups, 6, ROWS, LANES), F32),
            pltpu.VMEM((groups, 6, ROWS, LANES), F32),
            pltpu.VMEM((modes, groups, ROWS, LANES), F32),
            pltpu.VMEM((modes, groups, ROWS, LANES), F32),
            pltpu.VMEM((groups, near, own, ROWS, LANES), F32),
            pltpu.VMEM((groups, near, own, ROWS, LANES), F32),
            pltpu.VMEM((groups, near, own, ROWS, LANES), F32),
            pltpu.VMEM((groups, own, ROWS, LANES), F32),
            pltpu.VMEM((groups, across, own, ROWS, LANES), F32),
            pltpu.VMEM((groups, near, own, ROWS, LANES), F32),
            pltpu.VMEM((groups, near, own, ROWS, LANES), F32),
            pltpu.VMEM((PAIR * ROWS, LANES), F32),
            pltpu.VMEM((length, width), projected.dtype),
            dma((groups, 3)),
            dma((4,)),
            dma((groups,)),
            dma,
            dma,
            dma((groups,)),
            dma((groups,)),
            dma((groups,)),
            dma((groups,)),
            dma((groups,)),
            dma((groups,)),
            dma((groups, across - 1)),
            dma((groups, across)),
            dma((groups,)),
            dma((groups,)),
        ],
        compiler_params=pltpu.CompilerParams(
            collective_id=0, has_side_effects=True, vmem_limit_bytes=48 * 1024 * 1024
        ),
        name="hyena",
    )(projected, *[pltpu.with_memory_space_constraint(v, pltpu.HBM) for v in (short_filter, residues, decays, skip[None])])


def solution(mesh):
    return jax.shard_map(
        functools.partial(shards, mesh.shape["chan"], mesh.shape["seq"]),
        mesh=mesh,
        in_specs=(
            P(None, ("chan", "seq"), None),
            P(),
            P(None, ("chan", "seq")),
            P(None, ("chan", "seq")),
            P(("chan", "seq")),
        ),
        out_specs=P(("chan", "seq"), None),
        check_vma=False,
    )
```

```python
import functools

import jax
import jax.numpy as jnp
from jax import lax
from jax.experimental import pallas as pl
from jax.experimental.pallas import tpu as pltpu
from jax.sharding import PartitionSpec as P

LANES = 128
ROWS = 8
WIDE = LANES * ROWS
BLOCK = 8
PAIR = 16
PIECES = 2
MESH = pl.DeviceIdType.MESH
F32 = jnp.float32


SIDE = 4


def hops(*steps):
    return sum(min(step, SIDE - step) for step in steps)


CHIPS = sorted(
    [(dy, dx, dz) for dy in range(SIDE) for dx in range(SIDE) for dz in range(SIDE)][1:],
    key=lambda steps: -hops(*steps),
)
NEAR = sorted(
    [(dz, dk) for dz in range(SIDE) for dk in range(2)][1:],
    key=lambda steps: -hops(steps[0]) - steps[1] / 2,
)
ACROSS = sorted(
    [(dy, dx) for dy in range(SIDE) for dx in range(SIDE)][1:], key=lambda steps: -hops(*steps)
)


def token(t):
    return pl.ds((t // ROWS) * ROWS * ROWS + t % ROWS, ROWS, stride=ROWS)


def kernel(
    n_chan,
    n_seq,
    x_hbm,
    filt_hbm,
    residues_hbm,
    rates_hbm,
    direct_hbm,
    out_hbm,
    xb,
    filt_rows,
    filt,
    residues,
    rates,
    direct,
    tiles,
    gated,
    queries,
    ends,
    params,
    weight,
    decay,
    skip,
    last,
    halo,
    head,
    power,
    power_block,
    state,
    got_state,
    before,
    total,
    got_total,
    back,
    carried,
    out_tiles,
    out_rows,
    in_sem,
    small_sem,
    out_sem,
    send_near,
    recv_near,
    send_far,
    recv_far,
    send_halo,
    recv_halo,
    send_state,
    recv_state,
    send_total,
    recv_total,
    send_back,
    recv_back,
):
    groups = gated.shape[0]
    length = x_hbm.shape[1]
    modes = weight.shape[0]
    my_chan = lax.axis_index("chan")
    my_seq = lax.axis_index("seq")
    count = n_chan * n_seq
    mine = my_chan * n_seq + my_seq
    after = lax.rem(mine + 1, count)
    ahead = lax.rem(mine + count - 1, count)
    chips = count // 2
    my_chip = mine // 2
    my_core = mine % 2
    other = 1 - my_core
    near = 2 * SIDE
    across = count // near
    own = modes // near
    my_near = mine % near
    my_across = mine // near
    plane = 2 * SIDE
    my_z = my_seq % plane // 2
    my_y = my_seq // plane * 2 + my_chan // SIDE
    my_x = my_chan % SIDE
    places_z = [lax.rem(my_z + d, SIDE) * 2 for d in range(SIDE)]
    places_x = [lax.rem(my_x + d, SIDE) for d in range(SIDE)]
    turned_y = [lax.rem(my_y + d, SIDE) for d in range(SIDE)]
    chan_y = [y % 2 * SIDE for y in turned_y]
    seq_y = [y // 2 * plane for y in turned_y]
    cores = [my_core, other]

    def device(dy=0, dx=0, dz=0, dk=0):
        return (chan_y[dy] + places_x[dx], seq_y[dy] + places_z[dz] + cores[dk])

    barrier = pltpu.get_barrier_semaphore()

    def signal(target):
        pl.semaphore_signal(barrier, inc=1, device_id=target, device_id_type=MESH)

    for steps in CHIPS:
        signal(device(*steps))
    crossing = [dz for dz, dk in NEAR if dk]
    for dz in crossing:
        signal(device(dz=dz, dk=1))
    signal((ahead // n_seq, ahead % n_seq))
    signals = len(CHIPS) + len(crossing) + 1

    def fetch(j, m):
        columns = pl.ds(m * WIDE, WIDE)
        return pltpu.make_async_copy(
            x_hbm.at[j, :, columns], xb.at[j, :, columns], in_sem.at[m, j]
        )

    small = [
        pltpu.make_async_copy(source, place, small_sem.at[i])
        for i, (source, place) in enumerate(
            [
                (residues_hbm, residues),
                (rates_hbm, rates),
                (direct_hbm, direct),
                (filt_hbm, filt_rows),
            ]
        )
    ]
    for copy in small:
        copy.start()
    for m in range(groups):
        for j in range(3):
            fetch(j, m).start()

    for copy in small:
        copy.wait()
    for j in range(3):
        for tap in range(3):
            for m in range(groups):
                for i in range(ROWS):
                    lanes = slice(m * WIDE + i * LANES, m * WIDE + (i + 1) * LANES)
                    filt[3 * j + tap, m, i : i + 1, :] = filt_rows[j, tap : tap + 1, lanes]

    part = residues.shape[1]
    quads = LANES // part
    half = modes // quads
    for r in range(half):
        for b in range(quads):
            n = r * quads + b
            lanes = slice(b * part, (b + 1) * part)
            params[my_core, my_chip, r, :, lanes] = residues[n : n + 1, :] * jnp.sqrt(rates[n : n + 1, :])
            params[my_core, my_chip, half + r, :, lanes] = rates[n : n + 1, :]
    params[my_core, my_chip, 2 * half, :, 0:part] = direct[...]
    params[my_core, my_chip, 2 * half, :, part:] = jnp.zeros((1, LANES - part), F32)

    def near_copy(steps):
        place = params.at[my_core, my_chip]
        return pltpu.make_async_remote_copy(
            src_ref=place,
            dst_ref=place,
            send_sem=send_near,
            recv_sem=recv_near,
            device_id=device(*steps),
            device_id_type=MESH,
        )

    def wait_near(sem):
        some = params.at[0, pl.ds(0, chips - 1)]
        pltpu.make_async_copy(some, some, sem).wait()

    def far_copy(m):
        place = params.at[my_core, pl.ds(m * (chips // groups), chips // groups)]
        return pltpu.make_async_remote_copy(
            src_ref=place,
            dst_ref=place,
            send_sem=send_far.at[m],
            recv_sem=recv_far.at[m],
            device_id=device(dk=1),
            device_id_type=MESH,
        )

    def halo_copy(m):
        return pltpu.make_async_remote_copy(
            src_ref=last.at[m],
            dst_ref=halo.at[m],
            send_sem=send_halo.at[m],
            recv_sem=recv_halo.at[m],
            device_id=(after // n_seq, after % n_seq),
            device_id_type=MESH,
        )

    def spread_params(m):
        far_copy(m).wait_recv()
        group = lax.broadcasted_iota(jnp.int32, (ROWS, LANES), 1) // part

        def pick(row):
            found = []
            for i in range(quads):
                found.append(
                    jnp.concatenate(
                        [
                            params[i % 2, ((m * ROWS + j) * quads + i) // 2, row, :, :]
                            for j in range(ROWS)
                        ],
                        axis=0,
                    )
                )
            return found

        def place(found, b):
            value = None
            for i in range(quads):
                shift = (i - b) % quads * part
                turned = pltpu.roll(found[i], shift, 1) if shift else found[i]
                value = turned if i == 0 else jnp.where(group == i, turned, value)
            return value

        for r in range(half):
            heavy = pick(r)
            rate = pick(half + r)
            for b in range(quads):
                n = r * quads + b
                weight[n, m] = place(heavy, b)
                value = place(rate, b)
                decay[n, m] = value
                power[n, m] = jnp.exp(-value)
                power_block[n, m] = jnp.exp(-float(BLOCK) * value)
        skip[m] = place(pick(2 * half), 0)

    def patch(m):
        halo_copy(m).wait_recv()
        for t in range(2):
            featured = []
            for j in range(3):
                rows = [
                    jnp.where(mine > 0, halo[m, 2 * j], 0.0),
                    jnp.where(mine > 0, halo[m, 2 * j + 1], 0.0),
                    head[m, 2 * j],
                    head[m, 2 * j + 1],
                ]
                featured.append(
                    filt[3 * j, m] * rows[t + 2]
                    + filt[3 * j + 1, m] * rows[t + 1]
                    + filt[3 * j + 2, m] * rows[t]
                )
            queries[m, t * ROWS : (t + 1) * ROWS, :] = featured[0]
            gated[m, t * ROWS : (t + 1) * ROWS, :] = featured[1] * featured[2]

    def feature(m):
        for j in range(3):
            fetch(j, m).wait()
        coefs = [[filt[3 * j + s, m] for s in range(3)] for j in range(3)]

        def step(b, olds):
            for j in range(3):
                rows = xb[j, pl.ds(pl.multiple_of(b * PAIR, PAIR), PAIR), m * WIDE : (m + 1) * WIDE]
                rows = rows.astype(F32)
                for h in range(PAIR // ROWS):
                    for i in range(ROWS):
                        at = (h * ROWS + i) * ROWS
                        tiles[j, at : at + ROWS, :] = rows[
                            h * ROWS : (h + 1) * ROWS, i * LANES : (i + 1) * LANES
                        ]
            olds = list(olds)
            for t in range(PAIR):
                featured = []
                for j in range(3):
                    now = tiles[j, token(t), :]
                    older, old = olds[2 * j], olds[2 * j + 1]
                    featured.append(coefs[j][0] * now + coefs[j][1] * old + coefs[j][2] * older)
                    olds[2 * j], olds[2 * j + 1] = old, now
                place = pl.ds(pl.multiple_of((b * PAIR + t) * ROWS, ROWS), ROWS)
                queries[m, place, :] = featured[0]
                gated[m, place, :] = featured[1] * featured[2]
            return tuple(olds)

        zero = jnp.zeros((ROWS, LANES), F32)
        olds = lax.fori_loop(0, length // PAIR, step, (zero,) * 6)
        for i in range(6):
            last[m, i] = olds[i]
        halo_copy(m).start()
        for j in range(3):
            rows = xb[j, 0:PAIR, m * WIDE : (m + 1) * WIDE].astype(F32)[:ROWS]
            for i in range(ROWS):
                tiles[j, i * ROWS : (i + 1) * ROWS, :] = rows[:, i * LANES : (i + 1) * LANES]
            for t in range(2):
                head[m, 2 * j + t] = tiles[j, token(t), :]

    def gather_states(m):
        some = modes // 2
        for part in range(0, modes, some):
            chosen = range(part, part + some)
            rate = [power[n, m] for n in chosen]
            rate_block = [power_block[n, m] for n in chosen]
            heavy = [weight[n, m] for n in chosen]

            def step(pair, states):
                for half in range(PAIR // BLOCK):
                    b = pair * (PAIR // BLOCK) + half
                    values = [
                        gated[m, pl.ds(pl.multiple_of((b * BLOCK + i) * ROWS, ROWS), ROWS), :]
                        for i in range(BLOCK)
                    ]
                    results = []
                    for k, n in enumerate(chosen):
                        end = values[0]
                        for i in range(1, BLOCK):
                            end = rate[k] * end + values[i]
                        end = heavy[k] * end
                        ends[m, b, n] = end
                        results.append(rate_block[k] * states[k] + end)
                    states = tuple(results)
                return states

            zero = jnp.zeros((ROWS, LANES), F32)
            states = lax.fori_loop(0, length // PAIR, step, (zero,) * some)
            for k, n in enumerate(chosen):
                state[m, n // own, n % own] = states[k]

    def state_copy(m, steps):
        dz, dk = steps
        target = device(dz=dz, dk=dk)
        peer = target[1] % near
        return pltpu.make_async_remote_copy(
            src_ref=state.at[m, peer],
            dst_ref=got_state.at[m, my_near],
            send_sem=send_state.at[m],
            recv_sem=recv_state.at[m],
            device_id=target,
            device_id_type=MESH,
        )

    def each_total(m, act):
        for i, steps in enumerate(ACROSS):
            target = device(*steps)
            copy = pltpu.make_async_remote_copy(
                src_ref=total.at[m],
                dst_ref=got_total.at[m, my_across],
                send_sem=send_total.at[m, i],
                recv_sem=recv_total.at[m, my_across],
                device_id=target,
                device_id_type=MESH,
            )

            @pl.when(target[0] * 2 + target[1] // near > my_across)
            def _():
                act(copy)

    def back_copy(m, steps):
        dz, dk = steps
        target = device(dz=dz, dk=dk)
        peer = target[1] % near
        return pltpu.make_async_remote_copy(
            src_ref=back.at[m, peer],
            dst_ref=carried.at[m, my_near],
            send_sem=send_back.at[m],
            recv_sem=recv_back.at[m],
            device_id=target,
            device_id_type=MESH,
        )

    def wait_bytes(ref, count, m, sem):
        some = ref.at[m, pl.ds(0, count)]
        pltpu.make_async_copy(some, some, sem.at[m]).wait()

    def send_states(m):
        for steps in NEAR:
            state_copy(m, steps).start()
        got_state[m, my_near] = state[m, my_near]

    def scan_group(m):
        wait_bytes(got_state, near - 1, m, recv_state)
        for u in range(own):
            shrink = jnp.exp(-float(length) * decay[my_near * own + u, m])
            running = jnp.zeros((ROWS, LANES), F32)
            for k in range(near):
                before[m, k, u] = running
                running = shrink * running + got_state[m, k, u]
            total[m, u] = running
        each_total(m, lambda copy: copy.start())

    def scan_all(m):
        for c in range(across - 1):
            place = got_total.at[m, c]
            arrival = pltpu.make_async_copy(place, place, recv_total.at[m, c])

            @pl.when(c < my_across)
            def _():
                arrival.wait()

        for u in range(own):
            rate = decay[my_near * own + u, m]
            shrink = jnp.exp(-float(length) * rate)
            shrink_group = jnp.exp(-float(length * near) * rate)
            running = jnp.zeros((ROWS, LANES), F32)
            for c in range(across - 1):
                running = jnp.where(
                    c < my_across, shrink_group * running + got_total[m, c, u], running
                )
            for k in range(near):
                back[m, k, u] = before[m, k, u] + running
                running = shrink * running
        for steps in NEAR:
            back_copy(m, steps).start()
        carried[m, my_near] = back[m, my_near]

    def write(m, piece):
        columns = pl.ds(m * WIDE, WIDE)
        rows = pl.ds(piece * (length // PIECES), length // PIECES)
        return pltpu.make_async_copy(
            out_rows.at[rows, columns], out_hbm.at[rows, columns], out_sem.at[m, piece]
        )

    def block_places(b):
        return [pl.ds(pl.multiple_of((b * BLOCK + i) * ROWS, ROWS), ROWS) for i in range(BLOCK)]

    def convolve_block(m):
        term = [weight[n, m] for n in range(modes)]
        taps = []
        for i in range(BLOCK):
            tap = term[0]
            for n in range(1, modes):
                tap = tap + term[n]
            taps.append(tap + skip[m] if i == 0 else tap)
            if i < BLOCK - 1:
                term = [term[n] * power[n, m] for n in range(modes)]

        def step(pair, _):
            for half in range(PAIR // BLOCK):
                places = block_places(pair * (PAIR // BLOCK) + half)
                values = [gated[m, places[i], :] for i in range(BLOCK)]
                for i in range(BLOCK):
                    one = taps[0] * values[i]
                    for j in range(1, i + 1):
                        one = one + taps[j] * values[i - j]
                    gated[m, places[i], :] = one
            return 0

        lax.fori_loop(0, length // PAIR, step, 0)

    def convolve(m):
        wait_bytes(carried, near - 1, m, recv_back)

        def step(pair, states):
            for half in range(PAIR // BLOCK):
                b = pair * (PAIR // BLOCK) + half
                places = block_places(b)
                sums = [gated[m, places[i], :] for i in range(BLOCK)]
                results = []
                for n in range(modes):
                    rate = power[n, m]
                    now = states[n]
                    for i in range(BLOCK):
                        now = now * rate
                        sums[i] = sums[i] + now
                    results.append(now + ends[m, b, n])
                states = tuple(results)
                for i in range(BLOCK):
                    out_tiles[token(half * BLOCK + i), :] = sums[i] * queries[m, places[i], :]
            for i in range(ROWS):
                parts = [
                    out_tiles[(h * ROWS + i) * ROWS : (h * ROWS + i + 1) * ROWS, :]
                    for h in range(PAIR // ROWS)
                ]
                lanes = m * WIDE + i * LANES
                out_rows[pl.ds(pl.multiple_of(pair * PAIR, PAIR), PAIR), lanes : lanes + LANES] = (
                    jnp.concatenate(parts, axis=0).astype(out_rows.dtype)
                )
            return states

        states = tuple(carried[m, n // own, n % own] for n in range(modes))
        steps = length // PAIR // PIECES
        for piece in range(PIECES):
            states = lax.fori_loop(piece * steps, (piece + 1) * steps, step, states)
            write(m, piece).start()

    pl.semaphore_wait(barrier, signals)
    for steps in CHIPS:
        near_copy(steps).start()
    for m in range(groups):
        feature(m)
    wait_near(recv_near)
    for m in range(groups):
        far_copy(m).start()
    def first(m):
        patch(m)
        spread_params(m)
        gather_states(m)
        send_states(m)

    steps = [(first, 0), (first, 1), (first, 2), (scan_group, 0), (first, 3)]
    steps += [(scan_group, 1), (convolve_block, 0), (scan_group, 2), (convolve_block, 1)]
    steps += [(scan_all, 0), (scan_group, 3), (convolve_block, 2), (scan_all, 1)]
    steps += [(convolve_block, 3), (scan_all, 2), (scan_all, 3)]
    steps += [(convolve, 0), (convolve, 1), (convolve, 2), (convolve, 3)]
    for act, m in steps:
        act(m)
    wait_near(send_near)
    for m in range(groups):
        for piece in range(PIECES):
            write(m, piece).wait()
        halo_copy(m).wait_send()
        far_copy(m).wait_send()
        wait_bytes(got_state, near - 1, m, send_state)
        each_total(m, lambda copy: copy.wait_send())
        wait_bytes(carried, near - 1, m, send_back)


def shards(n_chan, n_seq, projected, short_filter, residues, decays, skip):
    _, length, width = projected.shape
    modes = residues.shape[0]
    groups = width // WIDE
    hbm = pl.BlockSpec(memory_space=pltpu.HBM)
    dma = pltpu.SemaphoreType.DMA
    blocks = length // BLOCK
    near = 2 * SIDE
    across = n_chan * n_seq // near
    own = modes // near
    rows = 2 * modes * residues.shape[1] // LANES + 1
    return pl.pallas_call(
        functools.partial(kernel, n_chan, n_seq),
        out_shape=jax.ShapeDtypeStruct((length, width), projected.dtype),
        in_specs=[hbm] * 5,
        out_specs=pl.BlockSpec(memory_space=pl.ANY),
        scratch_shapes=[
            pltpu.VMEM((3, length, width), projected.dtype),
            pltpu.VMEM(short_filter.shape, F32),
            pltpu.VMEM((9, groups, ROWS, LANES), F32),
            pltpu.VMEM(residues.shape, F32),
            pltpu.VMEM(decays.shape, F32),
            pltpu.VMEM((1, skip.shape[0]), F32),
            pltpu.VMEM((3, PAIR * ROWS, LANES), F32),
            pltpu.VMEM((groups, length * ROWS, LANES), F32),
            pltpu.VMEM((groups, length * ROWS, LANES), F32),
            pltpu.VMEM((groups, blocks, modes, ROWS, LANES), F32),
            pltpu.VMEM((2, n_chan * n_seq // 2, rows, 1, LANES), F32),
            pltpu.VMEM((modes, groups, ROWS, LANES), F32),
            pltpu.VMEM((modes, groups, ROWS, LANES), F32),
            pltpu.VMEM((groups, ROWS, LANES), F32),
            pltpu.VMEM((groups, 6, ROWS, LANES), F32),
            pltpu.VMEM((groups, 6, ROWS, LANES), F32),
            pltpu.VMEM((groups, 6, ROWS, LANES), F32),
            pltpu.VMEM((modes, groups, ROWS, LANES), F32),
            pltpu.VMEM((modes, groups, ROWS, LANES), F32),
            pltpu.VMEM((groups, near, own, ROWS, LANES), F32),
            pltpu.VMEM((groups, near, own, ROWS, LANES), F32),
            pltpu.VMEM((groups, near, own, ROWS, LANES), F32),
            pltpu.VMEM((groups, own, ROWS, LANES), F32),
            pltpu.VMEM((groups, across, own, ROWS, LANES), F32),
            pltpu.VMEM((groups, near, own, ROWS, LANES), F32),
            pltpu.VMEM((groups, near, own, ROWS, LANES), F32),
            pltpu.VMEM((PAIR * ROWS, LANES), F32),
            pltpu.VMEM((length, width), projected.dtype),
            dma((groups, 3)),
            dma((4,)),
            dma((groups, PIECES)),
            dma,
            dma,
            dma((groups,)),
            dma((groups,)),
            dma((groups,)),
            dma((groups,)),
            dma((groups,)),
            dma((groups,)),
            dma((groups, across - 1)),
            dma((groups, across)),
            dma((groups,)),
            dma((groups,)),
        ],
        compiler_params=pltpu.CompilerParams(
            collective_id=0, has_side_effects=True, vmem_limit_bytes=48 * 1024 * 1024
        ),
        name="hyena",
    )(projected, *[pltpu.with_memory_space_constraint(v, pltpu.HBM) for v in (short_filter, residues, decays, skip[None])])


def solution(mesh):
    return jax.shard_map(
        functools.partial(shards, mesh.shape["chan"], mesh.shape["seq"]),
        mesh=mesh,
        in_specs=(
            P(None, ("chan", "seq"), None),
            P(),
            P(None, ("chan", "seq")),
            P(None, ("chan", "seq")),
            P(("chan", "seq")),
        ),
        out_specs=P(("chan", "seq"), None),
        check_vma=False,
    )
```

```python
import functools

import jax
import jax.numpy as jnp
from jax import lax
from jax.experimental import pallas as pl
from jax.experimental.pallas import tpu as pltpu
from jax.sharding import PartitionSpec as P

LANES = 128
ROWS = 8
WIDE = LANES * ROWS
BLOCK = 8
PAIR = 16
PIECES = 2
MESH = pl.DeviceIdType.MESH
F32 = jnp.float32


SIDE = 4


def hops(*steps):
    return sum(min(step, SIDE - step) for step in steps)


CHIPS = sorted(
    [(dy, dx, dz) for dy in range(SIDE) for dx in range(SIDE) for dz in range(SIDE)][1:],
    key=lambda steps: -hops(*steps),
)
NEAR = sorted(
    [(dz, dk) for dz in range(SIDE) for dk in range(2)][1:],
    key=lambda steps: -hops(steps[0]) - steps[1] / 2,
)
ACROSS = sorted(
    [(dy, dx) for dy in range(SIDE) for dx in range(SIDE)][1:], key=lambda steps: -hops(*steps)
)


def token(t):
    return pl.ds((t // ROWS) * ROWS * ROWS + t % ROWS, ROWS, stride=ROWS)


def kernel(
    n_chan,
    n_seq,
    x_hbm,
    filt_hbm,
    residues_hbm,
    rates_hbm,
    direct_hbm,
    out_hbm,
    xb,
    filt_rows,
    filt,
    residues,
    rates,
    direct,
    tiles,
    gated,
    queries,
    ends,
    params,
    weight,
    decay,
    skip,
    last,
    halo,
    head,
    power,
    power_block,
    state,
    got_state,
    before,
    total,
    got_total,
    back,
    carried,
    out_tiles,
    out_rows,
    in_sem,
    small_sem,
    out_sem,
    send_near,
    recv_near,
    send_far,
    recv_far,
    send_halo,
    recv_halo,
    send_state,
    recv_state,
    send_total,
    recv_total,
    send_back,
    recv_back,
):
    groups = gated.shape[0]
    length = x_hbm.shape[1]
    modes = weight.shape[0]
    my_chan = lax.axis_index("chan")
    my_seq = lax.axis_index("seq")
    count = n_chan * n_seq
    mine = my_chan * n_seq + my_seq
    after = lax.rem(mine + 1, count)
    ahead = lax.rem(mine + count - 1, count)
    chips = count // 2
    my_chip = mine // 2
    my_core = mine % 2
    other = 1 - my_core
    near = 2 * SIDE
    across = count // near
    own = modes // near
    my_near = mine % near
    my_across = mine // near
    plane = 2 * SIDE
    my_z = my_seq % plane // 2
    my_y = my_seq // plane * 2 + my_chan // SIDE
    my_x = my_chan % SIDE
    places_z = [lax.rem(my_z + d, SIDE) * 2 for d in range(SIDE)]
    places_x = [lax.rem(my_x + d, SIDE) for d in range(SIDE)]
    turned_y = [lax.rem(my_y + d, SIDE) for d in range(SIDE)]
    chan_y = [y % 2 * SIDE for y in turned_y]
    seq_y = [y // 2 * plane for y in turned_y]
    cores = [my_core, other]

    def device(dy=0, dx=0, dz=0, dk=0):
        return (chan_y[dy] + places_x[dx], seq_y[dy] + places_z[dz] + cores[dk])

    barrier = pltpu.get_barrier_semaphore()

    def signal(target):
        pl.semaphore_signal(barrier, inc=1, device_id=target, device_id_type=MESH)

    for steps in CHIPS:
        signal(device(*steps))
    crossing = [dz for dz, dk in NEAR if dk]
    for dz in crossing:
        signal(device(dz=dz, dk=1))
    signal((ahead // n_seq, ahead % n_seq))
    signals = len(CHIPS) + len(crossing) + 1

    def fetch(j, m):
        columns = pl.ds(m * WIDE, WIDE)
        return pltpu.make_async_copy(
            x_hbm.at[j, :, columns], xb.at[j, :, columns], in_sem.at[m, j]
        )

    small = [
        pltpu.make_async_copy(source, place, small_sem.at[i])
        for i, (source, place) in enumerate(
            [
                (residues_hbm, residues),
                (rates_hbm, rates),
                (direct_hbm, direct),
                (filt_hbm, filt_rows),
            ]
        )
    ]
    for copy in small:
        copy.start()
    for m in range(groups):
        for j in range(3):
            fetch(j, m).start()

    for copy in small:
        copy.wait()
    for j in range(3):
        for tap in range(3):
            for m in range(groups):
                for i in range(ROWS):
                    lanes = slice(m * WIDE + i * LANES, m * WIDE + (i + 1) * LANES)
                    filt[3 * j + tap, m, i : i + 1, :] = filt_rows[j, tap : tap + 1, lanes]

    part = residues.shape[1]
    quads = LANES // part
    half = modes // quads
    for r in range(half):
        for b in range(quads):
            n = r * quads + b
            lanes = slice(b * part, (b + 1) * part)
            params[my_core, my_chip, r, :, lanes] = residues[n : n + 1, :] * jnp.sqrt(rates[n : n + 1, :])
            params[my_core, my_chip, half + r, :, lanes] = rates[n : n + 1, :]
    params[my_core, my_chip, 2 * half, :, 0:part] = direct[...]
    params[my_core, my_chip, 2 * half, :, part:] = jnp.zeros((1, LANES - part), F32)

    def near_copy(steps):
        place = params.at[my_core, my_chip]
        return pltpu.make_async_remote_copy(
            src_ref=place,
            dst_ref=place,
            send_sem=send_near,
            recv_sem=recv_near,
            device_id=device(*steps),
            device_id_type=MESH,
        )

    def wait_near(sem):
        some = params.at[0, pl.ds(0, chips - 1)]
        pltpu.make_async_copy(some, some, sem).wait()

    def far_copy(m):
        place = params.at[my_core, pl.ds(m * (chips // groups), chips // groups)]
        return pltpu.make_async_remote_copy(
            src_ref=place,
            dst_ref=place,
            send_sem=send_far.at[m],
            recv_sem=recv_far.at[m],
            device_id=device(dk=1),
            device_id_type=MESH,
        )

    def halo_copy(m):
        return pltpu.make_async_remote_copy(
            src_ref=last.at[m],
            dst_ref=halo.at[m],
            send_sem=send_halo.at[m],
            recv_sem=recv_halo.at[m],
            device_id=(after // n_seq, after % n_seq),
            device_id_type=MESH,
        )

    def spread_params(m):
        far_copy(m).wait_recv()
        group = lax.broadcasted_iota(jnp.int32, (ROWS, LANES), 1) // part

        def pick(row):
            found = []
            for i in range(quads):
                found.append(
                    jnp.concatenate(
                        [
                            params[i % 2, ((m * ROWS + j) * quads + i) // 2, row, :, :]
                            for j in range(ROWS)
                        ],
                        axis=0,
                    )
                )
            return found

        def place(found, b):
            value = None
            for i in range(quads):
                shift = (i - b) % quads * part
                turned = pltpu.roll(found[i], shift, 1) if shift else found[i]
                value = turned if i == 0 else jnp.where(group == i, turned, value)
            return value

        for r in range(half):
            heavy = pick(r)
            rate = pick(half + r)
            for b in range(quads):
                n = r * quads + b
                weight[n, m] = place(heavy, b)
                value = place(rate, b)
                decay[n, m] = value
                power[n, m] = jnp.exp(-value)
                power_block[n, m] = jnp.exp(-float(BLOCK) * value)
        skip[m] = place(pick(2 * half), 0)

    def patch(m):
        halo_copy(m).wait_recv()
        for t in range(2):
            featured = []
            for j in range(3):
                rows = [
                    jnp.where(mine > 0, halo[m, 2 * j], 0.0),
                    jnp.where(mine > 0, halo[m, 2 * j + 1], 0.0),
                    head[m, 2 * j],
                    head[m, 2 * j + 1],
                ]
                featured.append(
                    filt[3 * j, m] * rows[t + 2]
                    + filt[3 * j + 1, m] * rows[t + 1]
                    + filt[3 * j + 2, m] * rows[t]
                )
            queries[m, t * ROWS : (t + 1) * ROWS, :] = featured[0]
            gated[m, t * ROWS : (t + 1) * ROWS, :] = featured[1] * featured[2]

    def feature(m):
        for j in range(3):
            fetch(j, m).wait()
        coefs = [[filt[3 * j + s, m] for s in range(3)] for j in range(3)]

        def step(b, olds):
            for j in range(3):
                rows = xb[j, pl.ds(pl.multiple_of(b * PAIR, PAIR), PAIR), m * WIDE : (m + 1) * WIDE]
                rows = rows.astype(F32)
                for h in range(PAIR // ROWS):
                    for i in range(ROWS):
                        at = (h * ROWS + i) * ROWS
                        tiles[j, at : at + ROWS, :] = rows[
                            h * ROWS : (h + 1) * ROWS, i * LANES : (i + 1) * LANES
                        ]
            olds = list(olds)
            for t in range(PAIR):
                featured = []
                for j in range(3):
                    now = tiles[j, token(t), :]
                    older, old = olds[2 * j], olds[2 * j + 1]
                    featured.append(coefs[j][0] * now + coefs[j][1] * old + coefs[j][2] * older)
                    olds[2 * j], olds[2 * j + 1] = old, now
                place = pl.ds(pl.multiple_of((b * PAIR + t) * ROWS, ROWS), ROWS)
                queries[m, place, :] = featured[0]
                gated[m, place, :] = featured[1] * featured[2]
            return tuple(olds)

        zero = jnp.zeros((ROWS, LANES), F32)
        olds = lax.fori_loop(0, length // PAIR, step, (zero,) * 6)
        for i in range(6):
            last[m, i] = olds[i]
        halo_copy(m).start()
        for j in range(3):
            rows = xb[j, 0:PAIR, m * WIDE : (m + 1) * WIDE].astype(F32)[:ROWS]
            for i in range(ROWS):
                tiles[j, i * ROWS : (i + 1) * ROWS, :] = rows[:, i * LANES : (i + 1) * LANES]
            for t in range(2):
                head[m, 2 * j + t] = tiles[j, token(t), :]

    def gather_states(m):
        some = modes // 2
        for part in range(0, modes, some):
            chosen = range(part, part + some)
            rate = [power[n, m] for n in chosen]
            rate_block = [power_block[n, m] for n in chosen]
            heavy = [weight[n, m] for n in chosen]

            def step(pair, states):
                for half in range(PAIR // BLOCK):
                    b = pair * (PAIR // BLOCK) + half
                    values = [
                        gated[m, pl.ds(pl.multiple_of((b * BLOCK + i) * ROWS, ROWS), ROWS), :]
                        for i in range(BLOCK)
                    ]
                    results = []
                    for k, n in enumerate(chosen):
                        end = values[0]
                        for i in range(1, BLOCK):
                            end = rate[k] * end + values[i]
                        end = heavy[k] * end
                        ends[m, b, n] = end
                        results.append(rate_block[k] * states[k] + end)
                    states = tuple(results)
                return states

            zero = jnp.zeros((ROWS, LANES), F32)
            states = lax.fori_loop(0, length // PAIR, step, (zero,) * some)
            for k, n in enumerate(chosen):
                state[m, n // own, n % own] = states[k]

    def state_copy(m, steps):
        dz, dk = steps
        target = device(dz=dz, dk=dk)
        peer = target[1] % near
        return pltpu.make_async_remote_copy(
            src_ref=state.at[m, peer],
            dst_ref=got_state.at[m, my_near],
            send_sem=send_state.at[m],
            recv_sem=recv_state.at[m],
            device_id=target,
            device_id_type=MESH,
        )

    def each_total(m, act):
        for i, steps in enumerate(ACROSS):
            target = device(*steps)
            copy = pltpu.make_async_remote_copy(
                src_ref=total.at[m],
                dst_ref=got_total.at[m, my_across],
                send_sem=send_total.at[m, i],
                recv_sem=recv_total.at[m, my_across],
                device_id=target,
                device_id_type=MESH,
            )

            @pl.when(target[0] * 2 + target[1] // near > my_across)
            def _():
                act(copy)

    def back_copy(m, steps):
        dz, dk = steps
        target = device(dz=dz, dk=dk)
        peer = target[1] % near
        return pltpu.make_async_remote_copy(
            src_ref=back.at[m, peer],
            dst_ref=carried.at[m, my_near],
            send_sem=send_back.at[m],
            recv_sem=recv_back.at[m],
            device_id=target,
            device_id_type=MESH,
        )

    def wait_bytes(ref, count, m, sem):
        some = ref.at[m, pl.ds(0, count)]
        pltpu.make_async_copy(some, some, sem.at[m]).wait()

    def send_states(m):
        for steps in NEAR:
            state_copy(m, steps).start()
        got_state[m, my_near] = state[m, my_near]

    def scan_group(m):
        wait_bytes(got_state, near - 1, m, recv_state)
        for u in range(own):
            shrink = jnp.exp(-float(length) * decay[my_near * own + u, m])
            running = jnp.zeros((ROWS, LANES), F32)
            for k in range(near):
                before[m, k, u] = running
                running = shrink * running + got_state[m, k, u]
            total[m, u] = running
        each_total(m, lambda copy: copy.start())

    def scan_all(m):
        for c in range(across - 1):
            place = got_total.at[m, c]
            arrival = pltpu.make_async_copy(place, place, recv_total.at[m, c])

            @pl.when(c < my_across)
            def _():
                arrival.wait()

        for u in range(own):
            rate = decay[my_near * own + u, m]
            shrink = jnp.exp(-float(length) * rate)
            shrink_group = jnp.exp(-float(length * near) * rate)
            running = jnp.zeros((ROWS, LANES), F32)
            for c in range(across - 1):
                running = jnp.where(
                    c < my_across, shrink_group * running + got_total[m, c, u], running
                )
            for k in range(near):
                back[m, k, u] = before[m, k, u] + running
                running = shrink * running
        for steps in NEAR:
            back_copy(m, steps).start()
        carried[m, my_near] = back[m, my_near]

    def write(m, piece):
        columns = pl.ds(m * WIDE, WIDE)
        rows = pl.ds(piece * (length // PIECES), length // PIECES)
        return pltpu.make_async_copy(
            out_rows.at[rows, columns], out_hbm.at[rows, columns], out_sem.at[m, piece]
        )

    def block_places(b):
        return [pl.ds(pl.multiple_of((b * BLOCK + i) * ROWS, ROWS), ROWS) for i in range(BLOCK)]

    def convolve_block(m):
        term = [weight[n, m] for n in range(modes)]
        taps = []
        for i in range(BLOCK):
            tap = term[0]
            for n in range(1, modes):
                tap = tap + term[n]
            taps.append(tap + skip[m] if i == 0 else tap)
            if i < BLOCK - 1:
                term = [term[n] * power[n, m] for n in range(modes)]

        def step(pair, _):
            for half in range(PAIR // BLOCK):
                places = block_places(pair * (PAIR // BLOCK) + half)
                values = [gated[m, places[i], :] for i in range(BLOCK)]
                for i in range(BLOCK):
                    one = taps[0] * values[i]
                    for j in range(1, i + 1):
                        one = one + taps[j] * values[i - j]
                    gated[m, places[i], :] = one
            return 0

        lax.fori_loop(0, length // PAIR, step, 0)

    def convolve(m):
        wait_bytes(carried, near - 1, m, recv_back)

        def step(pair, states):
            for half in range(PAIR // BLOCK):
                b = pair * (PAIR // BLOCK) + half
                places = block_places(b)
                sums = [gated[m, places[i], :] for i in range(BLOCK)]
                results = []
                for n in range(modes):
                    rate = power[n, m]
                    now = states[n]
                    for i in range(BLOCK):
                        now = now * rate
                        sums[i] = sums[i] + now
                    results.append(now + ends[m, b, n])
                states = tuple(results)
                for i in range(BLOCK):
                    out_tiles[token(half * BLOCK + i), :] = sums[i] * queries[m, places[i], :]
            for i in range(ROWS):
                parts = [
                    out_tiles[(h * ROWS + i) * ROWS : (h * ROWS + i + 1) * ROWS, :]
                    for h in range(PAIR // ROWS)
                ]
                lanes = m * WIDE + i * LANES
                out_rows[pl.ds(pl.multiple_of(pair * PAIR, PAIR), PAIR), lanes : lanes + LANES] = (
                    jnp.concatenate(parts, axis=0).astype(out_rows.dtype)
                )
            return states

        states = tuple(carried[m, n // own, n % own] for n in range(modes))
        steps = length // PAIR // PIECES
        for piece in range(PIECES):
            states = lax.fori_loop(piece * steps, (piece + 1) * steps, step, states)
            write(m, piece).start()

    pl.semaphore_wait(barrier, signals)
    for steps in CHIPS:
        near_copy(steps).start()
    for m in range(groups):
        feature(m)
    wait_near(recv_near)
    for m in range(groups):
        far_copy(m).start()
    def first(m):
        patch(m)
        spread_params(m)
        gather_states(m)
        send_states(m)

    steps = [(first, 0), (first, 1), (first, 2), (scan_group, 0), (first, 3)]
    steps += [(scan_group, 1), (convolve_block, 0), (scan_group, 2), (convolve_block, 1)]
    steps += [(scan_all, 0), (scan_group, 3), (scan_all, 1), (convolve_block, 2)]
    steps += [(scan_all, 2), (convolve_block, 3), (scan_all, 3)]
    steps += [(convolve, 0), (convolve, 1), (convolve, 2), (convolve, 3)]
    for act, m in steps:
        act(m)
    wait_near(send_near)
    for m in range(groups):
        for piece in range(PIECES):
            write(m, piece).wait()
        halo_copy(m).wait_send()
        far_copy(m).wait_send()
        wait_bytes(got_state, near - 1, m, send_state)
        each_total(m, lambda copy: copy.wait_send())
        wait_bytes(carried, near - 1, m, send_back)


def shards(n_chan, n_seq, projected, short_filter, residues, decays, skip):
    _, length, width = projected.shape
    modes = residues.shape[0]
    groups = width // WIDE
    hbm = pl.BlockSpec(memory_space=pltpu.HBM)
    dma = pltpu.SemaphoreType.DMA
    blocks = length // BLOCK
    near = 2 * SIDE
    across = n_chan * n_seq // near
    own = modes // near
    rows = 2 * modes * residues.shape[1] // LANES + 1
    return pl.pallas_call(
        functools.partial(kernel, n_chan, n_seq),
        out_shape=jax.ShapeDtypeStruct((length, width), projected.dtype),
        in_specs=[hbm] * 5,
        out_specs=pl.BlockSpec(memory_space=pl.ANY),
        scratch_shapes=[
            pltpu.VMEM((3, length, width), projected.dtype),
            pltpu.VMEM(short_filter.shape, F32),
            pltpu.VMEM((9, groups, ROWS, LANES), F32),
            pltpu.VMEM(residues.shape, F32),
            pltpu.VMEM(decays.shape, F32),
            pltpu.VMEM((1, skip.shape[0]), F32),
            pltpu.VMEM((3, PAIR * ROWS, LANES), F32),
            pltpu.VMEM((groups, length * ROWS, LANES), F32),
            pltpu.VMEM((groups, length * ROWS, LANES), F32),
            pltpu.VMEM((groups, blocks, modes, ROWS, LANES), F32),
            pltpu.VMEM((2, n_chan * n_seq // 2, rows, 1, LANES), F32),
            pltpu.VMEM((modes, groups, ROWS, LANES), F32),
            pltpu.VMEM((modes, groups, ROWS, LANES), F32),
            pltpu.VMEM((groups, ROWS, LANES), F32),
            pltpu.VMEM((groups, 6, ROWS, LANES), F32),
            pltpu.VMEM((groups, 6, ROWS, LANES), F32),
            pltpu.VMEM((groups, 6, ROWS, LANES), F32),
            pltpu.VMEM((modes, groups, ROWS, LANES), F32),
            pltpu.VMEM((modes, groups, ROWS, LANES), F32),
            pltpu.VMEM((groups, near, own, ROWS, LANES), F32),
            pltpu.VMEM((groups, near, own, ROWS, LANES), F32),
            pltpu.VMEM((groups, near, own, ROWS, LANES), F32),
            pltpu.VMEM((groups, own, ROWS, LANES), F32),
            pltpu.VMEM((groups, across, own, ROWS, LANES), F32),
            pltpu.VMEM((groups, near, own, ROWS, LANES), F32),
            pltpu.VMEM((groups, near, own, ROWS, LANES), F32),
            pltpu.VMEM((PAIR * ROWS, LANES), F32),
            pltpu.VMEM((length, width), projected.dtype),
            dma((groups, 3)),
            dma((4,)),
            dma((groups, PIECES)),
            dma,
            dma,
            dma((groups,)),
            dma((groups,)),
            dma((groups,)),
            dma((groups,)),
            dma((groups,)),
            dma((groups,)),
            dma((groups, across - 1)),
            dma((groups, across)),
            dma((groups,)),
            dma((groups,)),
        ],
        compiler_params=pltpu.CompilerParams(
            collective_id=0, has_side_effects=True, vmem_limit_bytes=48 * 1024 * 1024
        ),
        name="hyena",
    )(projected, *[pltpu.with_memory_space_constraint(v, pltpu.HBM) for v in (short_filter, residues, decays, skip[None])])


def solution(mesh):
    return jax.shard_map(
        functools.partial(shards, mesh.shape["chan"], mesh.shape["seq"]),
        mesh=mesh,
        in_specs=(
            P(None, ("chan", "seq"), None),
            P(),
            P(None, ("chan", "seq")),
            P(None, ("chan", "seq")),
            P(("chan", "seq")),
        ),
        out_specs=P(("chan", "seq"), None),
        check_vma=False,
    )
```
